32 devices in a mesh: seq: 8 (over z, x), head: 4 (over y, core).
Axes of the slice: x: 2, y: 2, z: 4, core: 2. Of those that a mesh axis runs over, the one named last changes fastest.
Arguments:
- layer_in: bfloat16 [2048, 2048], P('seq'), may hold values from -6 to 6
- out_grad: bfloat16 [2048, 2048], P('seq'), may hold values from -6 to 6
- doc_ids: int32 [2048], replicated, may hold values from 0 to 5, as said below
- attn_gain: bfloat16 [2048], P('seq'), may hold values from 0.5 to 1.5
- query_weight: bfloat16 [2048, 2048], P('seq', 'head'), may hold values from -0.125 to 0.125
- key_weight: bfloat16 [2048, 2048], P('seq', 'head'), may hold values from -0.125 to 0.125
- value_weight: bfloat16 [2048, 2048], P('seq', 'head'), may hold values from -0.125 to 0.125
- proj_weight: bfloat16 [2048, 2048], P('head', 'seq'), may hold values from -6 to 6
- mlp_gain: bfloat16 [2048], P('seq'), may hold values from 0.5 to 1.5
- gate_weight: bfloat16 [2048, 8192], P('seq', 'head'), may hold values from -0.125 to 0.125
- up_weight: bfloat16 [2048, 8192], P('seq', 'head'), may hold values from -0.125 to 0.125
- down_weight: bfloat16 [8192, 2048], P('head', 'seq'), may hold values from -0.0625 to 0.0625
Outputs:
- layer_out: bfloat16 [2048, 2048], P('seq')
- input_grad: float32 [2048, 2048], P('seq')
- grad_query: float32 [2048, 2048], P('seq', 'head')
- grad_key: float32 [2048, 2048], P('seq', 'head')
- grad_value: float32 [2048, 2048], P('seq', 'head')
- grad_proj: float32 [2048, 2048], P('head', 'seq')
- grad_gate: float32 [2048, 8192], P('seq', 'head')
- grad_up: float32 [2048, 8192], P('seq', 'head')
- grad_down: float32 [8192, 2048], P('head', 'seq')
- grad_attngain: float32 [2048], P('seq')
- grad_mlpgain: float32 [2048], P('seq')
The draws below stay inside these ranges and needn't reach their ends.
Inputs may be any that keep to these rules, and one draw needn't show every extreme that they name: `doc_ids`: document numbers start at 0 and rise by one at each boundary between documents; every boundary lies among the first 256 or the last 256 tokens of the sequence.
All inputs are finite; a program needn't handle non-finite values.
Results may differ from the reference program's by a relative error of at most 0.017.
Values may be sent and summed in bfloat16 or wider, within the bound.
No kernel may reach another device: no remote copies, remote signals or barrier semaphores. Data moves between devices by JAX's collectives and lax.ppermute only.
A program may use at most 192 MiB of HBM per device.

```python
import math
from functools import partial
import jax
import jax.numpy as jnp
from jax import lax

D = 2048
HD = 128
FF = 8192
TOK_DEV = 256
DOCS = 6
TOKENS = 2048


def draw_doc_ids(key, part):
    key = jax.random.fold_in(key, 7)
    key_count, key_left, key_right = jax.random.split(key, 3)
    cut_total = DOCS - 1
    left_count = jax.random.randint(key_count, (), 0, DOCS)
    left_cuts = jax.random.permutation(key_left, TOK_DEV - 1)[:cut_total] + 1
    right_cuts = jax.random.permutation(key_right, TOK_DEV - 1)[:cut_total] + (TOKENS - TOK_DEV + 1)
    cut_index = jnp.arange(cut_total, dtype=jnp.int32)
    left_live = cut_index < left_count
    right_live = cut_index < cut_total - left_count
    positions = jnp.arange(TOKENS, dtype=jnp.int32)
    left_hits = (left_live[None, :] & (left_cuts[None, :] <= positions[:, None])).astype(jnp.int32)
    right_hits = (right_live[None, :] & (right_cuts[None, :] <= positions[:, None])).astype(jnp.int32)
    return (jnp.sum(left_hits, axis=1) + jnp.sum(right_hits, axis=1)).astype(jnp.int32)


def shard_levels(own_key, shape, shards, smallest, largest):
    def one(position, shards_of):
        steps = jax.random.uniform(jax.random.fold_in(jax.random.fold_in(own_key, 6), position), (shards_of,), jnp.float32, smallest / len(shards), largest / len(shards))
        return jnp.repeat(jnp.exp(steps), shape[position] // shards_of).reshape((-1,) + (1,) * (len(shape) - position - 1))

    factor_of = one(*shards[0])
    for cut in shards[1:]:
        factor_of = factor_of * one(*cut)
    return factor_of


def bell_draw(own_key, shape, deviation, limit, cuts=(), held_as=jnp.bfloat16):
    array = jax.random.normal(own_key, shape, jnp.float32) * deviation
    if len(cuts) > 0:
        array = shard_levels(own_key, shape, cuts, -0.22, 0.18) * array
    return jnp.clip(array, min=-limit, max=limit).astype(held_as)


def setup_inputs(seed: int = 0) -> dict:
    arg_keys = jax.random.split(jax.random.key(seed), 13)
    return {
        "layer_in": bell_draw(arg_keys[0], (TOKENS, D), 1.0, 6.0, ((0, 8),)),
        "out_grad": bell_draw(arg_keys[1], (TOKENS, D), 1.0, 6.0, ((0, 8),)),
        "doc_ids": draw_doc_ids(jax.random.fold_in(arg_keys[12], 71), 0),
        "attn_gain": jnp.clip(1.0 + 0.1 * jax.random.normal(arg_keys[3], (D,), jnp.float32), 0.5, 1.5).astype(jnp.bfloat16),
        "query_weight": bell_draw(arg_keys[4], (D, D), D ** -0.5, 0.125, ((0, 8), (1, 4))),
        "key_weight": bell_draw(arg_keys[5], (D, D), D ** -0.5, 0.125, ((0, 8), (1, 4))),
        "value_weight": bell_draw(arg_keys[6], (D, D), D ** -0.5, 0.125, ((0, 8), (1, 4))),
        "proj_weight": bell_draw(arg_keys[7], (D, D), (max(D * TOKENS // 4194304, 1)) ** -0.5, 6.0, ((0, 4), (1, 8))),
        "mlp_gain": jnp.clip(1.0 + 0.1 * jax.random.normal(arg_keys[8], (D,), jnp.float32), 0.5, 1.5).astype(jnp.bfloat16),
        "gate_weight": bell_draw(arg_keys[9], (D, FF), D ** -0.5, 0.125, ((0, 8), (1, 4))),
        "up_weight": bell_draw(arg_keys[10], (D, FF), D ** -0.5, 0.125, ((0, 8), (1, 4))),
        "down_weight": bell_draw(arg_keys[11], (FF, D), FF ** -0.5, 0.0625, ((0, 4), (1, 8))),
    }


EPSILON = 1e-05
ROPE_BASE = 10000.0
LOG_BIAS = math.log(4096.0)
HIGHEST = lax.Precision.HIGHEST

@jax.custom_vjp
def low(v):
    return lax.optimization_barrier(v.astype(jnp.bfloat16)).astype(jnp.float32)

@jax.custom_vjp
def low_back(v):
    return v

def low_keep(v):
    return (low(v), None)

def low_pass(kept, grad):
    return (grad,)

def back_keep(v):
    return (v, None)

def back_low(kept, grad):
    return (low(grad),)
low.defvjp(low_keep, low_pass)
low_back.defvjp(back_keep, back_low)

def rope_tables(positions, width):
    half_width = width // 2
    frequency = ROPE_BASE ** (-jnp.arange(half_width, dtype=jnp.float32) * 2.0 / width)
    angles = positions.astype(jnp.float32)[:, None] * frequency[None, :]
    return (jnp.cos(angles), jnp.sin(angles))

def rotate(values, cosine, sine_tab):
    half_width = values.shape[-1] // 2
    leading = values[..., :half_width]
    trailing = values[..., half_width:]
    cos_rows = cosine[:, None, :]
    sin_rows = sine_tab[:, None, :]
    return jnp.concatenate([leading * cos_rows - trailing * sin_rows, trailing * cos_rows + leading * sin_rows], axis=-1)

def matmul(left_mat, right_mat):
    return jnp.dot(left_mat, right_mat, precision=HIGHEST, preferred_element_type=jnp.float32)

def rms_norm(values):
    return values * lax.rsqrt(lax.optimization_barrier(jnp.mean(values * values, axis=-1, keepdims=True)) + EPSILON)

def attention(query_rot, key_rot, value_low, doc_ids):
    total_rows = query_rot.shape[0]
    row_block = math.gcd(512, total_rows)
    positions = jnp.arange(total_rows, dtype=jnp.int32)
    scaling = query_rot.shape[-1] ** (-0.5)

    def one_block(block_index):
        first_row = block_index * row_block
        query_blk = lax.dynamic_slice_in_dim(query_rot, first_row, row_block, 0)
        query_pos = lax.dynamic_slice_in_dim(positions, first_row, row_block, 0)
        query_doc = lax.dynamic_slice_in_dim(doc_ids, first_row, row_block, 0)
        raw_scores = jnp.einsum('qhd,khd->hqk', query_blk, key_rot, precision=HIGHEST)
        scores = low_back(raw_scores * scaling - LOG_BIAS)
        live_mask = (query_doc[:, None] == doc_ids[None, :]) & (query_pos[:, None] >= positions[None, :])
        prob_vals = low(jnp.where(live_mask[None], jax.nn.sigmoid(scores), 0.0))
        return jnp.einsum('hqk,khd->qhd', prob_vals, value_low, precision=HIGHEST)
    outputs = lax.map(jax.checkpoint(one_block), jnp.arange(total_rows // row_block, dtype=jnp.int32))
    return outputs.reshape(query_rot.shape)

def layer(doc_ids, inputs, attn_gain, query_weight, key_weight, value_weight, proj_weight, mlp_gain, gate_weight, up_weight, down_weight):
    total_rows = inputs.shape[0]
    head_count = query_weight.shape[1] // HD
    positions = jnp.arange(total_rows, dtype=jnp.int32)
    cosine, sine_tab = rope_tables(positions, HD)
    hidden_a = low(rms_norm(inputs) * attn_gain)
    query_raw = low_back(matmul(hidden_a, query_weight)).reshape(total_rows, head_count, HD)
    key_raw = low_back(matmul(hidden_a, key_weight)).reshape(total_rows, head_count, HD)
    value_low = low_back(low(matmul(hidden_a, value_weight))).reshape(total_rows, head_count, HD)
    query_rot = low(rotate(query_raw, cosine, sine_tab))
    key_rot = low(rotate(key_raw, cosine, sine_tab))
    attended = attention(query_rot, key_rot, value_low, doc_ids).reshape(total_rows, head_count * HD)
    attended = low_back(low(attended))
    middle = inputs + low_back(matmul(attended, proj_weight))
    hidden_b = low(rms_norm(middle) * mlp_gain)
    gate_val = low_back(matmul(hidden_b, gate_weight))
    up_val = low_back(matmul(hidden_b, up_weight))
    active = low(jax.nn.silu(gate_val) * up_val)
    return middle + low_back(matmul(active, down_weight))

def reference(layer_in, out_grad, doc_ids, attn_gain, query_weight, key_weight, value_weight, proj_weight, mlp_gain, gate_weight, up_weight, down_weight):
    as_float = jnp.float32
    output, pullback = jax.vjp(partial(layer, doc_ids), layer_in.astype(as_float), attn_gain.astype(as_float), query_weight.astype(as_float), key_weight.astype(as_float), value_weight.astype(as_float), proj_weight.astype(as_float), mlp_gain.astype(as_float), gate_weight.astype(as_float), up_weight.astype(as_float), down_weight.astype(as_float))
    gradients = pullback(out_grad.astype(as_float))
    return (output.astype(jnp.bfloat16), gradients[0], gradients[2], gradients[3], gradients[4], gradients[5], gradients[7], gradients[8], gradients[9], gradients[1], gradients[6])
```

```python
import math

import jax
import jax.numpy as jnp
from jax import lax
from jax.sharding import PartitionSpec as P

HD = 128
EPSILON = 1e-05
ROPE_BASE = 10000.0
LOG_BIAS = math.log(4096.0)
LOW = jnp.bfloat16
F32 = jnp.float32


def dot(left_mat, right_mat):
    return lax.dot_general(
        left_mat, right_mat, (((1,), (0,)), ((), ())), preferred_element_type=F32
    )


def dot_last(left_mat, right_mat):
    return lax.dot_general(
        left_mat, right_mat, (((1,), (1,)), ((), ())), preferred_element_type=F32
    )


def dot_first(left_mat, right_mat):
    return lax.dot_general(
        left_mat, right_mat, (((0,), (0,)), ((), ())), preferred_element_type=F32
    )


def inv_rms(values):
    return lax.rsqrt(jnp.mean(values * values, axis=-1, keepdims=True) + EPSILON)


def norm_back(grad_normed, normed, inv_root):
    return inv_root * (
        grad_normed - normed * jnp.mean(grad_normed * normed, axis=-1, keepdims=True)
    )


def rope_tables(positions, width):
    half_width = width // 2
    frequency = ROPE_BASE ** (-jnp.arange(half_width, dtype=F32) * 2.0 / width)
    angles = positions.astype(F32)[:, None] * frequency[None, :]
    return (jnp.cos(angles), jnp.sin(angles))


def rotate(values, cosine, sine_tab):
    half_width = values.shape[-1] // 2
    leading = values[:, :half_width]
    trailing = values[:, half_width:]
    return jnp.concatenate(
        [leading * cosine - trailing * sine_tab, trailing * cosine + leading * sine_tab], axis=-1
    )


def pick(stacked, index):
    return lax.dynamic_index_in_dim(stacked, index, 0, keepdims=False)


def local(
    layer_in,
    out_grad,
    doc_ids,
    attn_gain,
    query_weight,
    key_weight,
    value_weight,
    proj_weight,
    mlp_gain,
    gate_weight,
    up_weight,
    down_weight,
):
    tok, width = layer_in.shape
    seq_size, head_size = lax.axis_size("seq"), lax.axis_size("head")
    far = query_weight.shape[1] // HD
    groups = seq_size // far
    own = tok // head_size
    seq_at, head_at = lax.axis_index("seq"), lax.axis_index("head")
    far_at, group_at = seq_at // groups, seq_at % groups
    rows_s = width // seq_size

    def far_swap(value, step):
        return lax.ppermute(
            value,
            "seq",
            [
                (i * groups + g, (i ^ step) * groups + g)
                for i in range(far)
                for g in range(groups)
            ],
        )

    def group_shift(value, step):
        return lax.ppermute(
            value,
            "seq",
            [
                (i * groups + g, i * groups + (g + step) % groups)
                for i in range(far)
                for g in range(groups)
            ],
        )

    def head_swap(value, step):
        return lax.ppermute(value, "head", [(i, i ^ step) for i in range(head_size)])

    def gather_rows(piece):
        gathered = jnp.stack([piece] + [far_swap(piece, k) for k in range(1, far)])
        gathered = jnp.stack([gathered, head_swap(gathered, 2)], axis=1)
        gathered = jnp.stack([gathered, head_swap(gathered, 1)], axis=2)
        return gathered.reshape(far * head_size * own, piece.shape[1])

    def scatter_rows(partial):
        partial = partial.astype(LOW).reshape(far, 2, 2, own, partial.shape[1])
        partial = partial[:, :, 0].astype(F32) + head_swap(partial[:, :, 1], 1).astype(F32)
        partial = partial.astype(LOW)
        partial = partial[:, 0].astype(F32) + head_swap(partial[:, 1], 2).astype(F32)
        partial = partial.astype(LOW)
        total = partial[0].astype(F32)
        for k in range(1, far):
            total = total + far_swap(partial[k], k).astype(F32)
        return total

    def to_absolute(value):
        parts = value.reshape(far * head_size, own, value.shape[1])
        return jnp.concatenate(
            [
                pick(parts, (i ^ far_at) * head_size + (j ^ head_at))
                for i in range(far)
                for j in range(head_size)
            ]
        )

    to_relative = to_absolute

    def spread_weight(blocks):
        got = [pick(blocks, far_at)] + [
            far_swap(pick(blocks, far_at ^ k), k) for k in range(1, far)
        ]
        got = jnp.stack(got)
        got = jnp.stack([pick(got, i ^ far_at) for i in range(far)])
        every = jnp.stack([got] + [group_shift(got, g) for g in range(1, groups)])
        return jnp.stack([pick(every, (group_at - g) % groups) for g in range(groups)], axis=1).reshape(
            (seq_size,) + blocks.shape[1:]
        )

    def collect_grad(blocks):
        blocks = blocks.reshape((far, groups) + blocks.shape[1:])

        def column(at):
            return lax.dynamic_index_in_dim(blocks, at, 1, keepdims=False)

        total = column(group_at)
        for g in range(1, groups):
            total = total + group_shift(column((group_at + g) % groups).astype(LOW), g).astype(F32)
        sent = total.astype(LOW)
        got = [pick(sent, far_at)] + [far_swap(pick(sent, far_at ^ k), k) for k in range(1, far)]
        got = jnp.stack(got)
        return [pick(got, i ^ far_at).astype(F32) for i in range(far)]

    gain_a = attn_gain.astype(F32)[:, None]
    gain_b = mlp_gain.astype(F32)[:, None]

    def gained(weight, gain):
        return (weight.astype(F32) * gain).astype(LOW)

    qkv_local = jnp.stack(
        [gained(w, gain_a).reshape(rows_s, far, HD) for w in (query_weight, key_weight, value_weight)],
        axis=2,
    )
    qkv_full = spread_weight(
        qkv_local.reshape(rows_s, far, 3 * HD).transpose(1, 0, 2)
    ).reshape(width, 3 * HD)
    cols_s = proj_weight.shape[1]
    proj_full = (
        spread_weight(proj_weight.reshape(far, HD, cols_s)).transpose(1, 0, 2).reshape(HD, width)
    )
    hidden = gate_weight.shape[1] // far

    def spread_columns(weight):
        return spread_weight(
            gained(weight, gain_b).reshape(rows_s, far, hidden).transpose(1, 0, 2)
        ).reshape(width, hidden)

    gate_full = spread_columns(gate_weight)
    up_full = spread_columns(up_weight)
    down_full = (
        spread_weight(down_weight.reshape(far, hidden, cols_s))
        .transpose(1, 0, 2)
        .reshape(hidden, width)
    )

    own_in = lax.dynamic_slice_in_dim(layer_in, head_at * own, own, 0).astype(F32)
    own_grad = lax.dynamic_slice_in_dim(out_grad, head_at * own, own, 0)
    inv_a = inv_rms(own_in)
    normed_a = own_in * inv_a
    hidden_a = gather_rows(normed_a.astype(LOW))
    qkv = to_absolute(dot(hidden_a, qkv_full))
    tok_group = far * tok
    row_ids = jnp.arange(tok, dtype=jnp.int32)
    far_ids = jnp.arange(far, dtype=jnp.int32)
    query_pos = ((far_ids * groups + group_at)[:, None] * tok + row_ids[None, :]).reshape(tok_group)
    cosine, sine_tab = rope_tables(query_pos, HD)
    query_rot = rotate(qkv[:, :HD], cosine, sine_tab).astype(LOW)
    key_value = jnp.concatenate(
        [rotate(qkv[:, HD : 2 * HD], cosine, sine_tab).astype(LOW), qkv[:, 2 * HD :].astype(LOW)],
        axis=1,
    ).reshape(far, tok, 2 * HD)
    key_value = jnp.stack(
        [key_value] + [group_shift(key_value, g) for g in range(1, groups)], axis=1
    )
    source = (group_at - jnp.arange(groups, dtype=jnp.int32)) % groups
    docs = doc_ids.reshape(far, groups, tok)
    query_doc = lax.dynamic_index_in_dim(docs, group_at, 1, keepdims=False)
    key_doc = jnp.stack(
        [lax.dynamic_index_in_dim(docs, source[g], 1, keepdims=False) for g in range(groups)], axis=1
    )
    key_pos = (far_ids[:, None] * groups + source[None, :])[:, :, None] * tok + row_ids
    query_pos = query_pos.reshape(far, tok)
    query_blocks = query_rot.reshape(far, tok, HD)
    scaling = HD**-0.5
    probs, keys, values, attended = [], [], [], []
    for i in range(far):
        key_blk = key_value[: i + 1, :, :, :HD].reshape(-1, HD)
        value_blk = key_value[: i + 1, :, :, HD:].reshape(-1, HD)
        live_mask = (query_doc[i][:, None] == key_doc[: i + 1].reshape(-1)[None, :]) & (
            query_pos[i][:, None] >= key_pos[: i + 1].reshape(-1)[None, :]
        )
        scores = dot_last(query_blocks[i], key_blk) * scaling - LOG_BIAS
        prob_vals = jnp.where(live_mask, jax.nn.sigmoid(scores), 0.0)
        keys.append(key_blk)
        values.append(value_blk)
        probs.append(prob_vals)
        attended.append(dot(prob_vals.astype(LOW), value_blk))
    attn_low = to_relative(jnp.concatenate(attended).astype(LOW))
    middle = own_in + scatter_rows(dot(attn_low, proj_full))

    inv_b = inv_rms(middle)
    normed_b = middle * inv_b
    grad_top = gather_rows(own_grad)
    hidden_b = gather_rows(normed_b.astype(LOW))
    gate_val = dot(hidden_b, gate_full)
    up_val = dot(hidden_b, up_full)
    gate_sig = jax.nn.sigmoid(gate_val)
    silu_val = gate_val * gate_sig
    active = (silu_val * up_val).astype(LOW)
    grad_active = dot_last(grad_top, down_full)
    grad_gate_val = (grad_active * up_val * gate_sig * (1.0 + gate_val * (1.0 - gate_sig))).astype(LOW)
    grad_up_val = (grad_active * silu_val).astype(LOW)
    grad_normed_b = scatter_rows(
        dot_last(grad_gate_val, gate_full) + dot_last(grad_up_val, up_full)
    )
    grad_middle = own_grad.astype(F32) + norm_back(grad_normed_b, normed_b, inv_b)
    out_rows = (middle + scatter_rows(dot(active, down_full))).astype(LOW)

    def merge_columns(blocks):
        return jnp.concatenate(blocks, axis=1)

    grad_gate = merge_columns(
        collect_grad(dot_first(hidden_b, grad_gate_val).reshape(seq_size, rows_s, hidden))
    )
    grad_up = merge_columns(
        collect_grad(dot_first(hidden_b, grad_up_val).reshape(seq_size, rows_s, hidden))
    )
    grad_down = jnp.concatenate(
        collect_grad(
            dot_first(active, grad_top).reshape(hidden, seq_size, cols_s).transpose(1, 0, 2)
        )
    )

    grad_mix = gather_rows(grad_middle.astype(LOW))
    grad_proj = jnp.concatenate(
        collect_grad(
            dot_first(attn_low, grad_mix).reshape(HD, seq_size, cols_s).transpose(1, 0, 2)
        )
    )
    grad_attn = to_absolute(dot_last(grad_mix, proj_full).astype(LOW)).reshape(far, tok, HD)
    grad_query, grad_keys, grad_values = [], None, None
    for i in reversed(range(far)):
        prob_low = probs[i].astype(LOW)
        value_term = dot_first(prob_low, grad_attn[i])
        grad_probs = dot_last(grad_attn[i], values[i])
        grad_scores = (grad_probs * probs[i] * (1.0 - probs[i])).astype(LOW)
        grad_query.insert(0, dot(grad_scores, keys[i]) * scaling)
        key_term = dot_first(grad_scores, query_blocks[i]) * scaling
        if grad_keys is None:
            grad_keys, grad_values = key_term, value_term
        else:
            count = key_term.shape[0]
            grad_keys = jnp.concatenate([grad_keys[:count] + key_term, grad_keys[count:]])
            grad_values = jnp.concatenate([grad_values[:count] + value_term, grad_values[count:]])
    grad_kv = jnp.concatenate([grad_keys, grad_values], axis=1).reshape(far, groups, tok, 2 * HD)
    total_kv = grad_kv[:, 0]
    for g in range(1, groups):
        total_kv = total_kv + group_shift(grad_kv[:, g].astype(LOW), groups - g).astype(F32)
    total_kv = total_kv.reshape(tok_group, 2 * HD)
    grad_qkv = to_relative(
        jnp.concatenate(
            [
                rotate(jnp.concatenate(grad_query), cosine, -sine_tab).astype(LOW),
                rotate(total_kv[:, :HD], cosine, -sine_tab).astype(LOW),
                total_kv[:, HD:].astype(LOW),
            ],
            axis=1,
        )
    )
    grad_normed_a = scatter_rows(dot_last(grad_qkv, qkv_full))
    grad_in = (grad_middle + norm_back(grad_normed_a, normed_a, inv_a)).astype(LOW)
    qkv_blocks = collect_grad(dot_first(hidden_a, grad_qkv).reshape(seq_size, rows_s, 3 * HD))
    grad_query_w, grad_key_w, grad_value_w = (
        jnp.concatenate([b[:, n * HD : (n + 1) * HD] for b in qkv_blocks], axis=1) for n in range(3)
    )

    def every_row(piece):
        gathered = jnp.stack([piece, head_swap(piece, 2)])
        gathered = jnp.stack([gathered, head_swap(gathered, 1)], axis=1)
        gathered = gathered.reshape((head_size,) + piece.shape)
        return jnp.concatenate([pick(gathered, j ^ head_at) for j in range(head_size)])

    def head_sum(value):
        value = value + head_swap(value, 1)
        return value + head_swap(value, 2)

    def times(weight, grad):
        return jnp.sum(weight.astype(F32) * grad, axis=1)

    grad_attngain = head_sum(
        times(query_weight, grad_query_w)
        + times(key_weight, grad_key_w)
        + times(value_weight, grad_value_w)
    )
    grad_mlpgain = head_sum(times(gate_weight, grad_gate) + times(up_weight, grad_up))
    return (
        every_row(out_rows),
        every_row(grad_in).astype(F32),
        grad_query_w * gain_a,
        grad_key_w * gain_a,
        grad_value_w * gain_a,
        grad_proj,
        grad_gate * gain_b,
        grad_up * gain_b,
        grad_down,
        grad_attngain,
        grad_mlpgain,
    )


def solution(mesh):
    return jax.shard_map(
        local,
        mesh=mesh,
        in_specs=(
            P("seq", None),
            P("seq", None),
            P(),
            P("seq"),
            P("seq", "head"),
            P("seq", "head"),
            P("seq", "head"),
            P("head", "seq"),
            P("seq"),
            P("seq", "head"),
            P("seq", "head"),
            P("head", "seq"),
        ),
        out_specs=(
            P("seq", None),
            P("seq", None),
            P("seq", "head"),
            P("seq", "head"),
            P("seq", "head"),
            P("head", "seq"),
            P("seq", "head"),
            P("seq", "head"),
            P("head", "seq"),
            P("seq"),
            P("seq"),
        ),
        check_vma=False,
    )
```

```python
import functools
import math

import jax
import jax.numpy as jnp
from jax import lax
from jax.experimental import pallas as pl
from jax.experimental.pallas import tpu as pltpu
from jax.sharding import PartitionSpec as P

HD = 128
EPSILON = 1e-05
ROPE_BASE = 10000.0
LOG_BIAS = math.log(4096.0)
LOW = jnp.bfloat16
F32 = jnp.float32
G_ATTN_X = [("x0", "x1"), ("x0", "x1"), ("x0", "x2"), ("x0", "x2")]
G_TOP = (("start", "x0"), ("x2", "attend"), ("qkv", "z0"), ("z0", "z1"))
G_MLP_Z = [("x1", "x2"), ("x2", "z0"), ("kv", "z2")]
G_MLP_X = [("attend", "z2"), ("z1", "h1"), ("z2", "h2"), ("h0", "mlp")]
G_MLPG_X = [("turn", "r1"), ("m0", "m2"), ("g2", "m1"), ("g1", "m0")]
G_MLPG_Z = [("turn", "r2"), ("back", "r1"), ("m1", "turn")]
G_OUT = (("g1", "g2"), ("g2", "m0"), ("m0", "m1"), ("in", "end"))
G_ATTNG_X = [("r1", "in")] * 4
G_ATTNG_Z = [("in", "end")] * 3
VMEM_ASK = 40 * 1024 * 1024


def dot(left_mat, right_mat):
    return lax.dot_general(
        left_mat, right_mat, (((1,), (0,)), ((), ())), preferred_element_type=F32
    )


def dot_last(left_mat, right_mat):
    return lax.dot_general(
        left_mat, right_mat, (((1,), (1,)), ((), ())), preferred_element_type=F32
    )


def dot_first(left_mat, right_mat):
    return lax.dot_general(
        left_mat, right_mat, (((0,), (0,)), ((), ())), preferred_element_type=F32
    )


def inv_rms(values):
    return lax.rsqrt(jnp.mean(values * values, axis=-1, keepdims=True) + EPSILON)


def norm_back(grad_normed, normed, inv_root):
    return inv_root * (
        grad_normed - normed * jnp.mean(grad_normed * normed, axis=-1, keepdims=True)
    )


class Flow:
    def __init__(self):
        self.plans, self.got, self.due = {}, {}, {}

    def plan(self, name, start, end, make, send):
        self.plans.setdefault(start, []).append((name, end, make, send))

    def gate(self, label, values):
        values, ended = list(values), self.due.pop(label, [])
        planned = self.plans.pop(label, [])
        tied = list(
            lax.optimization_barrier(
                tuple(values) + tuple(ended) + tuple(make() for _, _, make, _ in planned)
            )
        )
        for (name, end, _, send), operand in zip(planned, tied[len(values) + len(ended) :]):
            result = self.got[name] = send(operand)
            self.due.setdefault(end, []).extend(result if isinstance(result, list) else [result])
        return tied[: len(values)]


def shape_of(rows, cols, kind):
    return jax.ShapeDtypeStruct((rows, cols), kind)


def at_rows(index, count):
    return pl.ds(pl.multiple_of(index * count, count), count)


SMEM_SPEC = pl.BlockSpec(memory_space=pltpu.SMEM)
ANY_SPEC = pl.BlockSpec(memory_space=pl.ANY)
VMEM_SPEC = pl.BlockSpec(memory_space=pltpu.VMEM)


def call(body, outs, scalars, arrays, scratch=(), space=VMEM_SPEC, flops=0):
    outs = tuple(outs)
    moved = sum(math.prod(a.shape) * a.dtype.itemsize for a in tuple(arrays) + outs)
    return pl.pallas_call(
        body,
        out_shape=outs,
        in_specs=[SMEM_SPEC] + [space] * len(arrays),
        out_specs=tuple([space] * len(outs)),
        scratch_shapes=list(scratch),
        compiler_params=pltpu.CompilerParams(vmem_limit_bytes=VMEM_ASK),
        cost_estimate=pl.CostEstimate(flops=flops, bytes_accessed=moved, transcendentals=0),
    )(scalars, *arrays)


def place(scalars, pieces, spots, rows, widths):
    count, many = len(pieces), len(widths)
    height = pieces[0].shape[0]

    def body(at, *refs):
        ins, outs, sems = refs[:count], refs[count:-1], refs[-1]
        copies = []
        for n in range(count):
            where, start = at_rows(spots[n](at), height), 0
            for m, breadth in enumerate(widths):
                copies.append(
                    pltpu.make_async_copy(
                        ins[n].at[:, start : start + breadth], outs[m].at[where, :], sems.at[n * many + m]
                    )
                )
                start += breadth
        for copy in copies:
            copy.start()
        for copy in copies:
            copy.wait()

    return call(
        body,
        [shape_of(rows, breadth, pieces[0].dtype) for breadth in widths],
        scalars,
        pieces,
        [pltpu.SemaphoreType.DMA((count * many,))],
        ANY_SPEC,
    )


def place_wide(scalars, pieces, spots, rows, cols, kind=F32):
    count = len(pieces)

    def body(at, *refs):
        out = refs[count]
        for n in range(count):
            out[at_rows(spots[n](at), pieces[n].shape[0]), :] = refs[n][...].astype(kind)

    return call(body, [shape_of(rows, cols, kind)], scalars, pieces)[0]


def finish_weights(scalars, pieces, weights, gain, spots):
    count, many = len(pieces), len(weights)
    height, breadth = weights[0].shape
    block = pieces[0].shape[1] // (many + 1)

    def body(at, *refs):
        ins, held, gains = refs[:count], refs[count : count + many], refs[count + many]
        outs, turned, terms = refs[count + many + 1 : -2], refs[-2], refs[-1]
        total = jnp.zeros((height, 1), F32)
        scale = gains[...]
        for n in range(count):
            where = at_rows(spots[n](at), block)
            for m in range(many):
                grad = ins[n][:, m * block : (m + 1) * block].astype(F32)
                outs[m][:, where] = grad * scale
                total += jnp.sum(grad * held[m][:, where].astype(F32), axis=1, keepdims=True)
            turned[where, :] = ins[n][:, many * block :].astype(F32).T
        terms[...] = total

    outs = [shape_of(height, breadth, F32) for _ in weights]
    outs += [shape_of(breadth, height, F32), shape_of(height, 1, F32)]
    return call(body, outs, scalars, list(pieces) + list(weights) + [gain])


def turn(values, cosine, signed):
    return values * cosine + pltpu.roll(values, HD // 2, 1) * signed


def piece_spots(far, head_size, own):
    for c in range(2):
        row = 0
        for first in (0, far // 2):
            for y in range(head_size // 2):
                for k in range(first, first + far // 2):
                    yield c, row, k, 2 * y + c
                    row += own


def rotate_all(scalars, chunks, cosine, signed, far, head_size, own):
    tok = own * head_size

    def body(at, low_ref, high_ref, cos_ref, sin_ref, query_ref, kv_ref):
        ins = (low_ref, high_ref)
        for c, row, k, m in piece_spots(far, head_size, own):
            spot = pl.ds(
                pl.multiple_of((at[0] ^ k) * tok + (at[1] ^ m) * own, own), own
            )
            cos_rows, sin_rows = cos_ref[spot, :], sin_ref[spot, :]
            value = ins[c][row : row + own, :]
            query_ref[spot, :] = turn(value[:, :HD], cos_rows, sin_rows).astype(LOW)
            kv_ref[spot, :HD] = turn(value[:, HD : 2 * HD], cos_rows, sin_rows).astype(LOW)
            kv_ref[spot, HD:] = value[:, 2 * HD :].astype(LOW)

    rows = far * tok
    return call(
        body,
        [shape_of(rows, HD, LOW), shape_of(rows, 2 * HD, LOW)],
        scalars,
        list(chunks) + [cosine, signed],
    )


def live_pairs(at, groups, far, tok):
    for i in range(far):
        for g in range(groups):
            for j in range(i + 1):
                yield i, g, j


def probabilities(at, query, key, query_doc, key_doc, i, g, j, groups):
    scores = lax.dot_general(query, key, (((1,), (1,)), ((), ())), preferred_element_type=F32)
    live = query_doc == key_doc
    if i == j:
        if g == 0:
            rows = lax.broadcasted_iota(jnp.int32, scores.shape, 0)
            cols = lax.broadcasted_iota(jnp.int32, scores.shape, 1)
            live = live & (rows >= cols)
        else:
            source = lax.rem(at[2] - g + groups, groups)
            live = live & (query_doc >= jnp.where(source < at[2], 0, 1 << 30))
    return jnp.where(live, jax.nn.sigmoid(scores * HD**-0.5 - LOG_BIAS), 0.0)


def attend(scalars, query, keys, query_doc, key_doc, far, head_size, own):
    tok, groups = own * head_size, len(keys)

    def body(at, query_ref, doc_ref, key_doc_ref, *refs):
        key_refs, (low_ref, high_ref, held) = refs[:groups], refs[groups:]
        for i in range(far):
            block = query_ref[i * tok : (i + 1) * tok, :]
            docs = doc_ref[i * tok : (i + 1) * tok, :]
            total = jnp.zeros((tok, HD), F32)
            for j in range(i + 1):
                for g in range(groups):
                    span = slice(j * tok, (j + 1) * tok)
                    probs = probabilities(
                        at, block, key_refs[g][span, :HD], docs, key_doc_ref[g : g + 1, span], i, g, j, groups
                    )
                    total += dot(probs.astype(LOW), key_refs[g][span, HD:])
            held[i * tok : (i + 1) * tok, :] = total.astype(LOW)
        outs = (low_ref, high_ref)
        for c, row, k, m in piece_spots(far, head_size, own):
            spot = pl.ds(
                pl.multiple_of((at[0] ^ k) * tok + (at[1] ^ m) * own, own), own
            )
            outs[c][row : row + own, :] = held[spot, :]

    rows = far * tok
    return call(
        body,
        [shape_of(rows // 2, HD, LOW)] * 2,
        scalars,
        [query, query_doc, key_doc] + list(keys),
        [pltpu.VMEM((rows, HD), LOW)],
        flops=4 * rows * rows * groups * HD // 2,
    )


def attend_back(scalars, query, keys, query_doc, key_doc, grads, far, head_size, own):
    tok, groups = own * head_size, len(keys)

    def body(at, query_ref, doc_ref, key_doc_ref, low_ref, high_ref, *refs):
        key_refs, outs, held = refs[:groups], refs[groups:-1], refs[-1]
        query_out, key_outs = outs[0], outs[1:]
        ins = (low_ref, high_ref)
        for c, row, k, m in piece_spots(far, head_size, own):
            spot = pl.ds(
                pl.multiple_of((at[0] ^ k) * tok + (at[1] ^ m) * own, own), own
            )
            held[spot, :] = ins[c][row : row + own, :]
        for j in range(far):
            for g in range(groups):
                span = slice(j * tok, (j + 1) * tok)
                key, value = key_refs[g][span, :HD], key_refs[g][span, HD:]
                key_total = jnp.zeros((tok, HD), F32)
                value_total = jnp.zeros((tok, HD), F32)
                for i in range(j, far):
                    rows = slice(i * tok, (i + 1) * tok)
                    block, grad = query_ref[rows, :], held[rows, :]
                    probs = probabilities(
                        at, block, key, doc_ref[rows, :], key_doc_ref[g : g + 1, span], i, g, j, groups
                    )
                    value_total += dot_first(probs.astype(LOW), grad)
                    terms = (dot_last(grad, value) * probs * (1.0 - probs)).astype(LOW)
                    key_total += dot_first(terms, block)
                    part = dot(terms, key) * HD**-0.5
                    if j == 0 and g == 0:
                        query_out[rows, :] = part
                    else:
                        query_out[rows, :] += part
                kind = key_outs[g].dtype
                key_outs[g][span, :HD] = (key_total * HD**-0.5).astype(kind)
                key_outs[g][span, HD:] = value_total.astype(kind)

    rows = far * tok
    return call(
        body,
        [shape_of(rows, HD, F32), shape_of(rows, 2 * HD, F32)]
        + [shape_of(rows, 2 * HD, LOW)] * (groups - 1),
        scalars,
        [query, query_doc, key_doc] + list(grads) + list(keys),
        [pltpu.VMEM((rows, HD), LOW)],
        flops=10 * rows * rows * groups * HD // 2,
    )


def rotate_back(scalars, query, keys, cosine, signed, far, head_size, own):
    tok, count = own * head_size, len(keys)

    def body(at, query_ref, cos_ref, sin_ref, *refs):
        key_refs, outs = refs[:count], refs[count:]
        for c, row, k, m in piece_spots(far, head_size, own):
            spot = pl.ds(
                pl.multiple_of((at[0] ^ k) * tok + (at[1] ^ m) * own, own), own
            )
            cos_rows, sin_rows = cos_ref[spot, :], -sin_ref[spot, :]
            total = key_refs[0][spot, :]
            for ref in key_refs[1:]:
                total += ref[spot, :].astype(F32)
            rows = slice(row, row + own)
            outs[c][rows, :HD] = turn(query_ref[spot, :], cos_rows, sin_rows).astype(LOW)
            outs[c][rows, HD : 2 * HD] = turn(total[:, :HD], cos_rows, sin_rows).astype(LOW)
            outs[c][rows, 2 * HD :] = total[:, HD:].astype(LOW)

    rows = far * tok
    return call(
        body,
        [shape_of(rows // 2, 3 * HD, LOW)] * 2,
        scalars,
        [query, cosine, signed] + list(keys),
    )


def local(
    layer_in,
    out_grad,
    doc_ids,
    attn_gain,
    query_weight,
    key_weight,
    value_weight,
    proj_weight,
    mlp_gain,
    gate_weight,
    up_weight,
    down_weight,
):
    tok, width = layer_in.shape
    seq_size, head_size = lax.axis_size("seq"), lax.axis_size("head")
    far = query_weight.shape[1] // HD
    groups = seq_size // far
    own = tok // head_size
    seq_at, head_at = lax.axis_index("seq"), lax.axis_index("head")
    far_at, group_at = seq_at // groups, seq_at % groups
    scalars = jnp.stack([far_at, head_at, group_at]).astype(jnp.int32)
    rows_s = width // seq_size
    hidden = gate_weight.shape[1] // far
    tok_group = far * tok

    def far_swap(value, step):
        return lax.ppermute(
            value,
            "seq",
            [(i * groups + g, (i ^ step) * groups + g) for i in range(far) for g in range(groups)],
        )

    def gather_far(piece):
        return [piece] + [far_swap(piece, k) for k in range(1, far)]

    def scatter_far(parts):
        total = parts[0].astype(F32)
        for k in reversed(range(1, far)):
            total = total + far_swap(parts[k].astype(LOW), k).astype(F32)
        return total

    def group_shift(value, step):
        return lax.ppermute(
            value,
            "seq",
            [
                (i * groups + g, i * groups + (g + step) % groups)
                for i in range(far)
                for g in range(groups)
            ],
        )

    def head_swap(value, step):
        return lax.ppermute(value, "head", [(i, i ^ step) for i in range(head_size)])

    flow = Flow()
    gate, plan, got = flow.gate, flow.plan, flow.got
    half_far = far // 2
    many_rows = half_far * own

    def core_swap(value):
        parts = [value[i : i + own] for i in range(0, value.shape[0], own)]
        return jnp.concatenate([head_swap(part, 1) for part in parts])

    def gather_rows(labels, piece):
        (piece,) = gate(labels[0], [piece])
        parts = gather_far(piece)
        near = jnp.concatenate(
            parts[:half_far] + [head_swap(part, 2) for part in parts[:half_far]]
        )
        rest = jnp.concatenate(parts[half_far:])
        near, rest = gate(labels[1], [near, rest])
        rest = jnp.concatenate([rest, head_swap(rest, 2)])
        near_got = core_swap(near)
        near, rest, near_got = gate(labels[2], [near, rest, near_got])
        return [
            jnp.concatenate([near, rest]),
            jnp.concatenate([near_got, core_swap(rest)]),
        ]

    def split_rows(chunks):
        return [[c[: 2 * many_rows], c[2 * many_rows :]] for c in chunks]

    def scatter_rows(labels, chunks):
        mine, other = split_rows(chunks)
        *mine, other[0], other[1] = gate(labels[0], mine + other)
        half = mine[1].astype(F32) + core_swap(other[1]).astype(F32)
        kept, sent, *left = gate(
            labels[1], [half[:many_rows], half[many_rows:].astype(LOW), mine[0], other[0]]
        )
        near = left[0].astype(F32) + core_swap(left[1]).astype(F32)
        rest = kept + head_swap(sent, 2).astype(F32)
        near, near_sent, rest = gate(
            labels[2], [near[:many_rows], near[many_rows:].astype(LOW), rest]
        )
        near = near + head_swap(near_sent, 2).astype(F32)
        return scatter_far(
            [part[k * own : (k + 1) * own] for part in (near, rest) for k in range(half_far)]
        )

    def plan_gather(tag, piece, far_gates, near_gates, rest_gates, core_gates):
        plan((tag, "far"), *far_gates, lambda: piece, gather_far)
        halves = (("near", range(half_far), near_gates), ("rest", range(half_far, far), rest_gates))
        for name, ks, gates in halves:
            plan(
                (tag, name),
                *gates,
                lambda ks=ks: jnp.concatenate([got[tag, "far"][k] for k in ks]),
                lambda v: head_swap(v, 2),
            )

            def both(name=name, ks=ks):
                return jnp.concatenate([got[tag, "far"][k] for k in ks] + [got[tag, name]])

            plan((tag, name, "core"), *core_gates, both, core_swap)

        def finish():
            parts = got[tag, "far"]
            mine = parts[:half_far] + [got[tag, "near"]] + parts[half_far:] + [got[tag, "rest"]]
            other = [got[tag, "near", "core"], got[tag, "rest", "core"]]
            return [jnp.concatenate(mine), jnp.concatenate(other)]

        return finish

    def plan_scatter(tag, chunks, core_gates, rest_gates, near_gates, far_gates):
        mine, other = split_rows(chunks)

        def half(n):
            return mine[n].astype(F32) + got[tag, "core", n].astype(F32)

        def part(k):
            n, at = k // half_far, k % half_far * own
            value = half(n)[:many_rows] + got[tag, "head", n].astype(F32)
            return value[at : at + own].astype(LOW)

        for n, gates in ((1, rest_gates), (0, near_gates)):
            plan((tag, "core", n), *core_gates, lambda n=n: other[n], core_swap)
            plan(
                (tag, "head", n),
                *gates,
                lambda n=n: half(n)[many_rows:].astype(LOW),
                lambda v: head_swap(v, 2),
            )
        plan(
            (tag, "far"),
            *far_gates,
            lambda: jnp.stack([part(k) for k in range(far)]),
            lambda v: scatter_far([v[k] for k in range(far)]),
        )
        return lambda: got[tag, "far"]

    steps = [(k, g) for k in range(far) for g in range(groups)]

    def source_of(k, g):
        return lambda at: (at[0] ^ k) * groups + lax.rem(at[2] + groups - g, groups)

    def plan_weights(tag, block_of, far_gates, group_gates):
        got[tag, 0, 0] = block_of(far_at)
        for k in range(far):
            if k:
                plan(
                    (tag, k, 0),
                    *far_gates[k],
                    lambda k=k: block_of(far_at ^ k),
                    lambda v, k=k: far_swap(v, k),
                )
            for g in range(1, groups):
                plan(
                    (tag, k, g),
                    *group_gates[k],
                    lambda k=k: got[tag, k, 0],
                    lambda v, g=g: group_shift(v, g),
                )

    def place_weights(tag, widths):
        pieces = [got[tag, k, g] for k, g in steps]
        return place(scalars, pieces, [source_of(*s) for s in steps], width, widths)

    def plan_grads(tag, grads, group_gates, far_gates):
        def rows(at):
            return jnp.concatenate(
                [lax.dynamic_slice_in_dim(v, at * rows_s, rows_s, 0) for v in grads], axis=1
            )

        def total(k):
            value = rows((far_at ^ k) * groups + group_at)
            for g in range(1, groups):
                value = value + got[tag, "x", k, g].astype(F32)
            return value.astype(LOW)

        for k in reversed(range(far)):
            for g in range(1, groups):
                plan(
                    (tag, "x", k, g),
                    *group_gates[k],
                    lambda k=k, g=g: rows((far_at ^ k) * groups + (group_at + g) % groups).astype(LOW),
                    lambda v, g=g: group_shift(v, g),
                )
            if k:
                plan((tag, k), *far_gates[k], lambda k=k: total(k), lambda v, k=k: far_swap(v, k))

        return lambda: [got[tag, k] if k else total(0) for k in range(far)]

    far_spots = [(lambda at, k=k: at[0] ^ k) for k in range(far)]
    head_spots = [(lambda at, m=m: at[1] ^ m) for m in (0, 2, 1, 3)]

    def every_row(piece):
        half = [piece, head_swap(piece, 2)]
        return half + [head_swap(part, 1) for part in half]

    def head_sum(value):
        value = value + head_swap(value, 1)
        return value + head_swap(value, 2)

    gain_a = attn_gain.astype(F32)[:, None]
    gain_b = mlp_gain.astype(F32)[:, None]

    def weight_block(weights, gain, turned, breadth):
        turned = turned.T

        def block_of(i):
            def columns(w):
                return lax.dynamic_slice_in_dim(w, i * breadth, breadth, 1)

            parts = [(columns(w).astype(F32) * gain).astype(LOW) for w in weights]
            return jnp.concatenate(parts + [columns(turned)], axis=1)

        return block_of

    own_in = lax.dynamic_slice_in_dim(layer_in, head_at * own, own, 0).astype(F32)
    own_grad = lax.dynamic_slice_in_dim(out_grad, head_at * own, own, 0)
    inv_a = inv_rms(own_in)
    normed_a = own_in * inv_a
    plan_weights(
        "attn",
        weight_block((query_weight, key_weight, value_weight), gain_a, proj_weight, HD),
        [None] + [("start", "x0")] * 3,
        G_ATTN_X,
    )
    finish_top = plan_gather(
        "top", own_grad, *G_TOP
    )
    plan_weights(
        "mlp",
        weight_block((gate_weight, up_weight), gain_b, down_weight, hidden),
        [None] + G_MLP_Z,
        G_MLP_X,
    )
    got["x"] = gate("start", [normed_a.astype(LOW)])[0]
    hidden_a = gather_rows(("x0", "x1", "x2"), got["x"])
    qkv_full, proj_turned = place_weights("attn", (3 * HD, HD))

    far_ids = jnp.arange(far, dtype=jnp.int32)
    positions = (far_ids * groups + group_at)[:, None] * tok + jnp.arange(tok, dtype=jnp.int32)
    frequency = ROPE_BASE ** (-jnp.arange(HD // 2, dtype=F32) * 2.0 / HD)
    angles = positions.reshape(tok_group).astype(F32)[:, None] * frequency[None, :]
    cosine, sine_tab = jnp.cos(angles), jnp.sin(angles)
    cosine = jnp.concatenate([cosine, cosine], axis=1)
    signed = jnp.concatenate([-sine_tab, sine_tab], axis=1)
    docs = doc_ids.reshape(far, groups, tok)
    query_doc = lax.dynamic_index_in_dim(docs, group_at, 1, keepdims=False).reshape(tok_group, 1)
    key_doc = jnp.stack(
        [
            lax.dynamic_index_in_dim(docs, (group_at - g) % groups, 1, keepdims=False).reshape(
                tok_group
            )
            for g in range(groups)
        ]
    )
    hidden_a = gate("qkv", hidden_a)
    query_rot, key_own = rotate_all(
        scalars, [dot(h, qkv_full) for h in hidden_a], cosine, signed, far, head_size, own
    )
    key_own, query_rot = gate("kv", [key_own, query_rot])
    keys = [key_own] + [group_shift(key_own, g) for g in range(1, groups)]

    query_rot, *keys = gate("attend", [query_rot] + keys)
    attn_low = attend(scalars, query_rot, keys, query_doc, key_doc, far, head_size, own)
    middle = own_in + scatter_rows(("z0", "z1", "z2"), [dot_last(a, proj_turned).astype(LOW) for a in attn_low])

    inv_b = inv_rms(middle)
    normed_b = middle * inv_b
    hidden_b = gather_rows(("h0", "h1", "h2"), normed_b.astype(LOW))
    hidden_b = gate("mlp", hidden_b)
    gate_up, down_turned = place_weights("mlp", (2 * hidden, hidden))
    grad_top = finish_top()
    active, grad_gu = [], []
    for h, top in zip(hidden_b, grad_top):
        gate_up_val = dot(h, gate_up)
        gate_val, up_val = gate_up_val[:, :hidden], gate_up_val[:, hidden:]
        gate_sig = jax.nn.sigmoid(gate_val)
        silu_val = gate_val * gate_sig
        active.append((silu_val * up_val).astype(LOW))
        grad_active = dot(top, down_turned)
        grad_gu.append(
            jnp.concatenate(
                [
                    (
                        grad_active * up_val * gate_sig * (1.0 + gate_val * (1.0 - gate_sig))
                    ).astype(LOW),
                    (grad_active * silu_val).astype(LOW),
                ],
                axis=1,
            )
        )
    def over_tokens(left_mats, right_mats):
        return sum(dot_first(a, b) for a, b in zip(left_mats, right_mats))

    grad_gu = gate("mlp done", grad_gu)
    finish_out = plan_scatter(
        "out",
        [dot_last(a, down_turned).astype(LOW) for a in active],
        *G_OUT,
    )
    finish_mlp = plan_grads(
        "mlp grads",
        [over_tokens(hidden_b, grad_gu), over_tokens(grad_top, active)],
        G_MLPG_X,
        [None] + G_MLPG_Z,
    )
    grad_normed_b = scatter_rows(
        ("g0", "g1", "g2"), [dot_last(g, gate_up).astype(LOW) for g in grad_gu]
    )
    grad_middle = own_grad.astype(F32) + norm_back(grad_normed_b, normed_b, inv_b)
    grad_mix = gather_rows(("m0", "m1", "m2"), grad_middle.astype(LOW))

    grad_mix = gate("back", grad_mix)
    grad_attn = [dot(g, proj_turned).astype(LOW) for g in grad_mix]
    grad_query, *grad_keys = attend_back(
        scalars, query_rot, keys, query_doc, key_doc, grad_attn, far, head_size, own
    )
    grad_query, *grad_keys = gate("kvb", [grad_query] + grad_keys)
    grad_keys = [grad_keys[0]] + [
        group_shift(grad_keys[g], groups - g) for g in range(1, groups)
    ]
    grad_query, *grad_keys = gate("turn", [grad_query] + grad_keys)
    grad_qkv = rotate_back(
        scalars, grad_query, grad_keys, cosine, signed, far, head_size, own
    )
    finish_attn = plan_grads(
        "attn grads",
        [over_tokens(hidden_a, grad_qkv), over_tokens(grad_mix, attn_low)],
        G_ATTNG_X,
        [None] + G_ATTNG_Z,
    )
    grad_normed_a = scatter_rows(
        ("r0", "r1", "r2"), [dot_last(g, qkv_full).astype(LOW) for g in grad_qkv]
    )
    grad_in = (grad_middle + norm_back(grad_normed_a, normed_a, inv_a)).astype(LOW)

    (grad_in,) = gate("in", [grad_in])
    in_rows = every_row(grad_in)
    in_rows = gate("end", in_rows)
    out_rows = every_row((middle + finish_out()).astype(LOW))
    grad_gate, grad_up, grad_down, mlp_terms = finish_weights(
        scalars, finish_mlp(), [gate_weight, up_weight], gain_b, far_spots
    )
    grad_query_w, grad_key_w, grad_value_w, grad_proj, attn_terms = finish_weights(
        scalars, finish_attn(), [query_weight, key_weight, value_weight], gain_a, far_spots
    )
    layer_out = place_wide(scalars, out_rows, head_spots, tok, width, LOW)
    input_grad = place_wide(scalars, in_rows, head_spots, tok, width)
    terms = head_sum(jnp.concatenate([attn_terms, mlp_terms], axis=1).T)
    return (
        layer_out,
        input_grad,
        grad_query_w,
        grad_key_w,
        grad_value_w,
        grad_proj,
        grad_gate,
        grad_up,
        grad_down,
        terms[0],
        terms[1],
    )


def solution(mesh):
    return jax.shard_map(
        local,
        mesh=mesh,
        in_specs=(
            P("seq", None),
            P("seq", None),
            P(),
            P("seq"),
            P("seq", "head"),
            P("seq", "head"),
            P("seq", "head"),
            P("head", "seq"),
            P("seq"),
            P("seq", "head"),
            P("seq", "head"),
            P("head", "seq"),
        ),
        out_specs=(
            P("seq", None),
            P("seq", None),
            P("seq", "head"),
            P("seq", "head"),
            P("seq", "head"),
            P("head", "seq"),
            P("seq", "head"),
            P("seq", "head"),
            P("head", "seq"),
            P("seq"),
            P("seq"),
        ),
        check_vma=False,
    )
```

```python
import functools
import math

import jax
import jax.numpy as jnp
from jax import lax
from jax.experimental import pallas as pl
from jax.experimental.pallas import tpu as pltpu
from jax.sharding import PartitionSpec as P

HD = 128
EPSILON = 1e-05
ROPE_BASE = 10000.0
LOG_BIAS = math.log(4096.0)
LOW = jnp.bfloat16
F32 = jnp.float32
G_ATTN = (("start", "x1"), ("x1", "x2"))
G_TOP = (("z1", "z2"), ("z2", "h1"), ("h0", "h2"))
G_MLP = (("x1", "z0"), ("z0", "h0"))
G_GRAD_MLP = (("g1n", "m2"), ("back", "r2"))
G_OUT = (("m0", "m1"), ("m1", "kvb"), ("m2", "kvb"), ("r2n", "end"))
G_GRAD_ATTN = (("r1n", "r2n"), ("r2n", "end"))
VMEM_ASK = 40 * 1024 * 1024


def dot(left_mat, right_mat):
    return lax.dot_general(
        left_mat, right_mat, (((1,), (0,)), ((), ())), preferred_element_type=F32
    )


def dot_last(left_mat, right_mat):
    return lax.dot_general(
        left_mat, right_mat, (((1,), (1,)), ((), ())), preferred_element_type=F32
    )


def dot_first(left_mat, right_mat):
    return lax.dot_general(
        left_mat, right_mat, (((0,), (0,)), ((), ())), preferred_element_type=F32
    )


def inv_rms(values):
    return lax.rsqrt(jnp.mean(values * values, axis=-1, keepdims=True) + EPSILON)


def norm_back(grad_normed, normed, inv_root):
    return inv_root * (
        grad_normed - normed * jnp.mean(grad_normed * normed, axis=-1, keepdims=True)
    )


class Flow:
    def __init__(self):
        self.plans, self.got, self.due = {}, {}, {}

    def plan(self, name, start, end, make, send):
        self.plans.setdefault(start, []).append((name, end, make, send))

    def gate(self, label, values):
        planned = self.plans.pop(label, [])
        names = self.due.pop(label, [])
        ended = [self.got[name] for name in names]
        values, ended, operands = lax.optimization_barrier(
            (list(values), ended, [make() for _, _, make, _ in planned])
        )
        self.got.update(zip(names, ended))
        for (name, end, _, send), operand in zip(planned, operands):
            self.got[name] = send(operand)
            self.due.setdefault(end, []).append(name)
        return values


def shape_of(rows, cols, kind):
    return jax.ShapeDtypeStruct((rows, cols), kind)


def at_rows(index, count):
    return pl.ds(pl.multiple_of(index * count, count), count)


SMEM_SPEC = pl.BlockSpec(memory_space=pltpu.SMEM)
ANY_SPEC = pl.BlockSpec(memory_space=pl.ANY)
VMEM_SPEC = pl.BlockSpec(memory_space=pltpu.VMEM)


def call(body, outs, scalars, arrays, scratch=(), space=VMEM_SPEC, flops=0):
    outs = tuple(outs)
    moved = sum(math.prod(a.shape) * a.dtype.itemsize for a in tuple(arrays) + outs)
    return pl.pallas_call(
        body,
        out_shape=outs,
        in_specs=[SMEM_SPEC] + [space] * len(arrays),
        out_specs=tuple([space] * len(outs)),
        scratch_shapes=list(scratch),
        compiler_params=pltpu.CompilerParams(vmem_limit_bytes=VMEM_ASK),
        cost_estimate=pl.CostEstimate(flops=flops, bytes_accessed=moved, transcendentals=0),
    )(scalars, *arrays)


def place(scalars, pieces, rows, height, breadth):
    count = len(pieces)
    blocks = pieces[0][0].shape[0] // height

    def body(at, *refs):
        ins, out, sems = refs[:count], refs[count], refs[count + 1]
        copies = []
        for n, (_, first, spot) in enumerate(pieces):
            for i in range(blocks):
                copies.append(
                    pltpu.make_async_copy(
                        ins[n].at[i * height : (i + 1) * height, first : first + breadth],
                        out.at[at_rows(spot(at, i), height), :],
                        sems.at[n * blocks + i],
                    )
                )
        for copy in copies:
            copy.start()
        for copy in copies:
            copy.wait()

    return call(
        body,
        [shape_of(rows, breadth, LOW)],
        scalars,
        [piece[0] for piece in pieces],
        [pltpu.SemaphoreType.DMA((count * blocks,))],
        ANY_SPEC,
    )[0]


def place_wide(scalars, pieces, spots, rows, cols, kind=F32):
    count = len(pieces)

    def body(at, *refs):
        out = refs[count]
        for n in range(count):
            out[at_rows(spots[n](at), pieces[n].shape[0]), :] = refs[n][...].astype(kind)

    return call(body, [shape_of(rows, cols, kind)], scalars, pieces)[0]


def finish_weights(scalars, pieces, weights, gain):
    many = len(weights)
    height, breadth = weights[0].shape
    count, block = pieces.shape[0], pieces.shape[2] // (many + 1)

    def body(at, piece_ref, *refs):
        held, gains = refs[:many], refs[many]
        outs, turned, terms = refs[many + 1 : -2], refs[-2], refs[-1]
        total = jnp.zeros((height, 1), F32)
        scale = gains[...]
        for i in range(count):
            where = slice(i * block, (i + 1) * block)
            for m in range(many):
                grad = piece_ref[i, :, m * block : (m + 1) * block].astype(F32)
                outs[m][:, where] = grad * scale
                total += jnp.sum(grad * held[m][:, where].astype(F32), axis=1, keepdims=True)
            turned[where, :] = piece_ref[i, :, many * block :].astype(F32).T
        terms[...] = total

    outs = [shape_of(height, breadth, F32) for _ in weights]
    outs += [shape_of(breadth, height, F32), shape_of(height, 1, F32)]
    return call(body, outs, scalars, [pieces] + list(weights) + [gain])


def turn(values, cosine, signed):
    return values * cosine + pltpu.roll(values, HD // 2, 1) * signed


def piece_spots(far, head_size, own):
    for c in range(2):
        row = 0
        for first in (0, far // 2):
            for y in range(head_size // 2):
                for k in range(first, first + far // 2):
                    yield c, row, k, 2 * y + c
                    row += own


def rotate_all(scalars, chunks, cosine, signed, far, head_size, own):
    tok = own * head_size

    def body(at, low_ref, high_ref, cos_ref, sin_ref, query_ref, kv_ref):
        ins = (low_ref, high_ref)
        for c, row, k, m in piece_spots(far, head_size, own):
            spot = pl.ds(
                pl.multiple_of((at[0] ^ k) * tok + (at[1] ^ m) * own, own), own
            )
            cos_rows, sin_rows = cos_ref[spot, :], sin_ref[spot, :]
            value = ins[c][row : row + own, :]
            query_ref[spot, :] = turn(value[:, :HD], cos_rows, sin_rows).astype(LOW)
            kv_ref[spot, :HD] = turn(value[:, HD : 2 * HD], cos_rows, sin_rows).astype(LOW)
            kv_ref[spot, HD:] = value[:, 2 * HD :].astype(LOW)

    rows = far * tok
    return call(
        body,
        [shape_of(rows, HD, LOW), shape_of(rows, 2 * HD, LOW)],
        scalars,
        list(chunks) + [cosine, signed],
    )


def live_pairs(at, groups, far, tok):
    for i in range(far):
        for g in range(groups):
            for j in range(i + 1):
                yield i, g, j


def probabilities(at, query, key, query_doc, key_doc, i, g, j, groups):
    scores = lax.dot_general(query, key, (((1,), (1,)), ((), ())), preferred_element_type=F32)
    live = query_doc == key_doc
    if i == j:
        if g == 0:
            rows = lax.broadcasted_iota(jnp.int32, scores.shape, 0)
            cols = lax.broadcasted_iota(jnp.int32, scores.shape, 1)
            live = live & (rows >= cols)
        else:
            source = lax.rem(at[2] - g + groups, groups)
            live = live & (query_doc >= jnp.where(source < at[2], 0, 1 << 30))
    return jnp.where(live, jax.nn.sigmoid(scores * HD**-0.5 - LOG_BIAS), 0.0)


def attend(scalars, query, keys, query_doc, key_doc, far, head_size, own):
    tok, groups = own * head_size, len(keys)

    def body(at, query_ref, doc_ref, key_doc_ref, *refs):
        key_refs, (low_ref, high_ref, held) = refs[:groups], refs[groups:]
        for i in range(far):
            block = query_ref[i * tok : (i + 1) * tok, :]
            docs = doc_ref[i * tok : (i + 1) * tok, :]
            total = jnp.zeros((tok, HD), F32)
            for j in range(i + 1):
                for g in range(groups):
                    span = slice(j * tok, (j + 1) * tok)
                    probs = probabilities(
                        at, block, key_refs[g][span, :HD], docs, key_doc_ref[g : g + 1, span], i, g, j, groups
                    )
                    total += dot(probs.astype(LOW), key_refs[g][span, HD:])
            held[i * tok : (i + 1) * tok, :] = total.astype(LOW)
        outs = (low_ref, high_ref)
        for c, row, k, m in piece_spots(far, head_size, own):
            spot = pl.ds(
                pl.multiple_of((at[0] ^ k) * tok + (at[1] ^ m) * own, own), own
            )
            outs[c][row : row + own, :] = held[spot, :]

    rows = far * tok
    return call(
        body,
        [shape_of(rows // 2, HD, LOW)] * 2,
        scalars,
        [query, query_doc, key_doc] + list(keys),
        [pltpu.VMEM((rows, HD), LOW)],
        flops=4 * rows * rows * groups * HD // 2,
    )


def attend_back(scalars, query, keys, query_doc, key_doc, grads, far, head_size, own):
    tok, groups = own * head_size, len(keys)

    def body(at, query_ref, doc_ref, key_doc_ref, low_ref, high_ref, *refs):
        key_refs, outs, held = refs[:groups], refs[groups:-1], refs[-1]
        query_out, key_outs = outs[0], outs[1:]
        ins = (low_ref, high_ref)
        for c, row, k, m in piece_spots(far, head_size, own):
            spot = pl.ds(
                pl.multiple_of((at[0] ^ k) * tok + (at[1] ^ m) * own, own), own
            )
            held[spot, :] = ins[c][row : row + own, :]
        for j in range(far):
            for g in range(groups):
                span = slice(j * tok, (j + 1) * tok)
                key, value = key_refs[g][span, :HD], key_refs[g][span, HD:]
                key_total = jnp.zeros((tok, HD), F32)
                value_total = jnp.zeros((tok, HD), F32)
                for i in range(j, far):
                    rows = slice(i * tok, (i + 1) * tok)
                    block, grad = query_ref[rows, :], held[rows, :]
                    probs = probabilities(
                        at, block, key, doc_ref[rows, :], key_doc_ref[g : g + 1, span], i, g, j, groups
                    )
                    value_total += dot_first(probs.astype(LOW), grad)
                    terms = (dot_last(grad, value) * probs * (1.0 - probs)).astype(LOW)
                    key_total += dot_first(terms, block)
                    part = dot(terms, key) * HD**-0.5
                    if j == 0 and g == 0:
                        query_out[rows, :] = part
                    else:
                        query_out[rows, :] += part
                kind = key_outs[g].dtype
                key_outs[g][span, :HD] = (key_total * HD**-0.5).astype(kind)
                key_outs[g][span, HD:] = value_total.astype(kind)

    rows = far * tok
    return call(
        body,
        [shape_of(rows, HD, F32), shape_of(rows, 2 * HD, F32)]
        + [shape_of(rows, 2 * HD, LOW)] * (groups - 1),
        scalars,
        [query, query_doc, key_doc] + list(grads) + list(keys),
        [pltpu.VMEM((rows, HD), LOW)],
        flops=10 * rows * rows * groups * HD // 2,
    )


def rotate_back(scalars, query, keys, cosine, signed, far, head_size, own):
    tok, count = own * head_size, len(keys)

    def body(at, query_ref, cos_ref, sin_ref, *refs):
        key_refs, outs = refs[:count], refs[count:]
        for c, row, k, m in piece_spots(far, head_size, own):
            spot = pl.ds(
                pl.multiple_of((at[0] ^ k) * tok + (at[1] ^ m) * own, own), own
            )
            cos_rows, sin_rows = cos_ref[spot, :], -sin_ref[spot, :]
            total = key_refs[0][spot, :]
            for ref in key_refs[1:]:
                total += ref[spot, :].astype(F32)
            rows = slice(row, row + own)
            outs[c][rows, :HD] = turn(query_ref[spot, :], cos_rows, sin_rows).astype(LOW)
            outs[c][rows, HD : 2 * HD] = turn(total[:, :HD], cos_rows, sin_rows).astype(LOW)
            outs[c][rows, 2 * HD :] = total[:, HD:].astype(LOW)

    rows = far * tok
    return call(
        body,
        [shape_of(rows // 2, 3 * HD, LOW)] * 2,
        scalars,
        [query, cosine, signed] + list(keys),
    )


def local(
    layer_in,
    out_grad,
    doc_ids,
    attn_gain,
    query_weight,
    key_weight,
    value_weight,
    proj_weight,
    mlp_gain,
    gate_weight,
    up_weight,
    down_weight,
):
    tok, width = layer_in.shape
    seq_size, head_size = lax.axis_size("seq"), lax.axis_size("head")
    far = query_weight.shape[1] // HD
    groups = seq_size // far
    own = tok // head_size
    seq_at, head_at = lax.axis_index("seq"), lax.axis_index("head")
    far_at, group_at = seq_at // groups, seq_at % groups
    scalars = jnp.stack([far_at, head_at, group_at]).astype(jnp.int32)
    rows_s = width // seq_size
    hidden = gate_weight.shape[1] // far
    tok_group = far * tok

    def far_swap(value, step):
        return lax.ppermute(
            value,
            "seq",
            [(i * groups + g, (i ^ step) * groups + g) for i in range(far) for g in range(groups)],
        )

    def gather_far(piece):
        return [piece] + [far_swap(piece, k) for k in range(1, far)]

    def scatter_far(parts):
        total = parts[0].astype(F32)
        for k in reversed(range(1, far)):
            total = total + far_swap(parts[k].astype(LOW), k).astype(F32)
        return total

    def far_exchange(blocks):
        return lax.all_to_all(
            blocks,
            "seq",
            0,
            0,
            axis_index_groups=[[i * groups + g for i in range(far)] for g in range(groups)],
            tiled=True,
        )

    def group_shift(value, step):
        return lax.ppermute(
            value,
            "seq",
            [
                (i * groups + g, i * groups + (g + step) % groups)
                for i in range(far)
                for g in range(groups)
            ],
        )

    def head_swap(value, step):
        return lax.ppermute(value, "head", [(i, i ^ step) for i in range(head_size)])

    flow = Flow()
    gate, plan, got = flow.gate, flow.plan, flow.got

    def keep(name, value, label):
        got[name] = value
        flow.due.setdefault(label, []).append(name)
    half_far = far // 2
    many_rows = half_far * own

    def core_swap(value):
        parts = [value[i : i + own] for i in range(0, value.shape[0], own)]
        return jnp.concatenate([head_swap(part, 1) for part in parts])

    def gather_rows(labels, piece):
        (piece,) = gate(labels[0], [piece])
        parts = gather_far(piece)
        near = jnp.concatenate(
            parts[:half_far] + [head_swap(part, 2) for part in parts[:half_far]]
        )
        (near,) = gate(labels[0] + "n", [near])
        rest = jnp.concatenate(parts[half_far:])
        near, rest = gate(labels[1], [near, rest])
        rest = jnp.concatenate([rest, head_swap(rest, 2)])
        near_got = core_swap(near)
        near, rest, near_got = gate(labels[2], [near, rest, near_got])
        return [
            jnp.concatenate([near, rest]),
            jnp.concatenate([near_got, core_swap(rest)]),
        ]

    def split_rows(chunks):
        return [[c[: 2 * many_rows], c[2 * many_rows :]] for c in chunks]

    def scatter_rows(labels, chunks):
        mine, other = split_rows(chunks)
        *mine, other[0], other[1] = gate(labels[0], mine + other)
        half = mine[1].astype(F32) + core_swap(other[1]).astype(F32)
        kept, sent, *left = gate(
            labels[1], [half[:many_rows], half[many_rows:].astype(LOW), mine[0], other[0]]
        )
        near = left[0].astype(F32) + core_swap(left[1]).astype(F32)
        (near,) = gate(labels[1] + "n", [near])
        rest = kept + head_swap(sent, 2).astype(F32)
        near, near_sent, rest = gate(
            labels[2], [near[:many_rows], near[many_rows:].astype(LOW), rest]
        )
        near = near + head_swap(near_sent, 2).astype(F32)
        (near,) = gate(labels[2] + "n", [near])
        return scatter_far(
            [part[k * own : (k + 1) * own] for part in (near, rest) for k in range(half_far)]
        )

    def plan_gather(tag, piece, far_gates, near_gates, rest_gates):
        plan((tag, "far"), *far_gates, lambda: piece, gather_far)
        halves = (("near", range(half_far), near_gates), ("rest", range(half_far, far), rest_gates))
        for name, ks, gates in halves:
            plan(
                (tag, name),
                *gates,
                lambda ks=ks: jnp.concatenate([got[tag, "far"][k] for k in ks]),
                lambda v: head_swap(v, 2),
            )

        def finish():
            parts = got[tag, "far"]
            mine = parts[:half_far] + [got[tag, "near"]] + parts[half_far:] + [got[tag, "rest"]]
            mine = jnp.concatenate(mine)
            return [mine, core_swap(mine)]

        return finish

    def plan_scatter(tag, chunks, core_gates, rest_gates, near_gates, far_gates):
        made = []

        def halves():
            if not made:
                made.extend(split_rows(chunks()))
            return made

        def half(n):
            mine = halves()[0]
            return mine[n].astype(F32) + got[tag, "core", n].astype(F32)

        def part(k):
            n, at = k // half_far, k % half_far * own
            value = half(n)[:many_rows] + got[tag, "head", n].astype(F32)
            return value[at : at + own].astype(LOW)

        for n, gates in ((1, rest_gates), (0, near_gates)):
            plan((tag, "core", n), *core_gates, lambda n=n: halves()[1][n], core_swap)
            plan(
                (tag, "head", n),
                *gates,
                lambda n=n: half(n)[many_rows:].astype(LOW),
                lambda v: head_swap(v, 2),
            )
        plan(
            (tag, "far"),
            *far_gates,
            lambda: jnp.stack([part(k) for k in range(far)]),
            lambda v: scatter_far([v[k] for k in range(far)]),
        )

    def column_blocks(weight, gain=None):
        breadth = weight.shape[1] // far
        blocks = [weight[:, i * breadth : (i + 1) * breadth] for i in range(far)]
        if gain is not None:
            blocks = [(block.astype(F32) * gain).astype(LOW) for block in blocks]
        return jnp.stack(blocks)

    def row_blocks(weight):
        return weight.reshape(far, weight.shape[0] // far, weight.shape[1]).transpose(0, 2, 1)

    def plan_weight(name, make, far_gates, group_gates):
        plan(name, *far_gates, make, far_exchange)
        for g in range(1, groups):
            plan((name, g), *group_gates, lambda: got[name], lambda v, g=g: group_shift(v, g))

    def place_weight(name, first, breadth):
        def flat(value):
            return value.reshape(-1, value.shape[2])

        def spot(g):
            return lambda at, i: i * groups + lax.rem(at[2] + groups - g, groups)

        pieces = [(flat(got[name]), first, spot(0))]
        pieces += [(flat(got[name, g]), first, spot(g)) for g in range(1, groups)]
        return place(scalars, pieces, width, rows_s, breadth)

    def plan_grad(name, make, group_gates, far_gates):
        made = []

        def part(at):
            if not made:
                made.extend(v.reshape(far, groups, rows_s, -1) for v in make())
            return jnp.concatenate(
                [lax.dynamic_index_in_dim(v, at, 1, keepdims=False) for v in made], axis=2
            )

        def total():
            value = part(group_at)
            for g in range(1, groups):
                value = value + got[name, "group", g].astype(F32)
            return value.astype(LOW)

        for g in range(1, groups):
            plan(
                (name, "group", g),
                *group_gates,
                lambda g=g: part((group_at + g) % groups).astype(LOW),
                lambda v, g=g: group_shift(v, g),
            )
        plan(name, *far_gates, total, far_exchange)

    head_spots = [(lambda at, m=m: at[1] ^ m) for m in (0, 2, 1, 3)]

    def every_row(piece):
        half = [piece, head_swap(piece, 2)]
        return half + [head_swap(part, 1) for part in half]

    def head_sum(value):
        value = value + head_swap(value, 1)
        return value + head_swap(value, 2)

    gain_a = attn_gain.astype(F32)[:, None]
    gain_b = mlp_gain.astype(F32)[:, None]

    own_in = lax.dynamic_slice_in_dim(layer_in, head_at * own, own, 0).astype(F32)
    own_grad = lax.dynamic_slice_in_dim(out_grad, head_at * own, own, 0)
    inv_a = inv_rms(own_in)
    normed_a = own_in * inv_a
    plan_weight(
        "attn",
        lambda: jnp.concatenate(
            [column_blocks(w, gain_a) for w in (query_weight, key_weight, value_weight)]
            + [row_blocks(proj_weight)],
            axis=2,
        ),
        *G_ATTN,
    )
    plan_weight(
        "mlp",
        lambda: jnp.concatenate(
            [column_blocks(w, gain_b) for w in (gate_weight, up_weight)] + [row_blocks(down_weight)],
            axis=2,
        ),
        *G_MLP,
    )
    finish_top = plan_gather("top", own_grad, *G_TOP)
    gate("start", [])
    hidden_a = gather_rows(("x0", "x1", "x2"), normed_a.astype(LOW))
    qkv_full, proj_turned = place_weight("attn", 0, 3 * HD), place_weight("attn", 3 * HD, HD)

    far_ids = jnp.arange(far, dtype=jnp.int32)
    positions = (far_ids * groups + group_at)[:, None] * tok + jnp.arange(tok, dtype=jnp.int32)
    frequency = ROPE_BASE ** (-jnp.arange(HD // 2, dtype=F32) * 2.0 / HD)
    angles = positions.reshape(tok_group).astype(F32)[:, None] * frequency[None, :]
    cosine, sine_tab = jnp.cos(angles), jnp.sin(angles)
    cosine = jnp.concatenate([cosine, cosine], axis=1)
    signed = jnp.concatenate([-sine_tab, sine_tab], axis=1)
    docs = doc_ids.reshape(far, groups, tok)
    query_doc = lax.dynamic_index_in_dim(docs, group_at, 1, keepdims=False).reshape(tok_group, 1)
    key_doc = jnp.stack(
        [
            lax.dynamic_index_in_dim(docs, (group_at - g) % groups, 1, keepdims=False).reshape(
                tok_group
            )
            for g in range(groups)
        ]
    )
    hidden_a = gate("qkv", hidden_a)
    query_rot, key_own = rotate_all(
        scalars, [dot(h, qkv_full) for h in hidden_a], cosine, signed, far, head_size, own
    )
    key_own, query_rot = gate("kv", [key_own, query_rot])
    keys = [key_own] + [group_shift(key_own, g) for g in range(1, groups)]

    query_rot, *keys = gate("attend", [query_rot] + keys)
    attn_low = attend(scalars, query_rot, keys, query_doc, key_doc, far, head_size, own)
    middle = own_in + scatter_rows(("z0", "z1", "z2"), [dot_last(a, proj_turned).astype(LOW) for a in attn_low])

    inv_b = inv_rms(middle)
    normed_b = middle * inv_b
    hidden_b = gather_rows(("h0", "h1", "h2"), normed_b.astype(LOW))
    hidden_b = gate("mlp", hidden_b)
    gate_up = place_weight("mlp", 0, 2 * hidden)
    down_turned = place_weight("mlp", 2 * hidden, hidden)
    parts, active = [], []
    for h in hidden_b:
        gate_up_val = dot(h, gate_up)
        gate_val, up_val = gate_up_val[:, :hidden], gate_up_val[:, hidden:]
        gate_sig = jax.nn.sigmoid(gate_val)
        silu_val = gate_val * gate_sig
        active.append((silu_val * up_val).astype(LOW))
        parts.append(
            (silu_val, up_val * gate_sig * (1.0 + gate_val * (1.0 - gate_sig)))
        )
    plan_scatter(
        "out", lambda: [dot_last(a, down_turned).astype(LOW) for a in active], *G_OUT
    )
    parts = gate("mlpb", [parts])[0]
    parts = gate("mlpc", [parts])[0]
    grad_top = finish_top()
    grad_gu = []
    for top, (silu_val, gate_slope) in zip(grad_top, parts):
        grad_active = dot(top, down_turned)
        grad_gu.append(
            jnp.concatenate(
                [(grad_active * gate_slope).astype(LOW), (grad_active * silu_val).astype(LOW)],
                axis=1,
            )
        )

    def over_tokens(left_mats, right_mats):
        return sum(dot_first(a, b) for a, b in zip(left_mats, right_mats))

    keep("mlp kept", (hidden_b, grad_gu, grad_top, active), "g1")

    def mlp_grads():
        hidden_b, grad_gu, grad_top, active = got["mlp kept"]
        return [over_tokens(hidden_b, grad_gu), over_tokens(grad_top, active)]

    plan_grad("mlp grads", mlp_grads, *G_GRAD_MLP)
    grad_normed_b = scatter_rows(
        ("g0", "g1", "g2"),
        [
            dot_last(g, gate_up).astype(LOW) for g in grad_gu
        ],
    )
    grad_middle = own_grad.astype(F32) + norm_back(grad_normed_b, normed_b, inv_b)
    grad_mix = gather_rows(("m0", "m1", "m2"), grad_middle.astype(LOW))

    grad_mix = gate("back", grad_mix)
    grad_attn = [dot(g, proj_turned).astype(LOW) for g in grad_mix]
    grad_query, *grad_keys = attend_back(
        scalars, query_rot, keys, query_doc, key_doc, grad_attn, far, head_size, own
    )
    grad_query, *grad_keys = gate("kvb", [grad_query] + grad_keys)
    grad_keys = [grad_keys[0]] + [
        group_shift(grad_keys[g], groups - g) for g in range(1, groups)
    ]
    grad_query, *grad_keys = gate("turn", [grad_query] + grad_keys)
    grad_qkv = rotate_back(
        scalars, grad_query, grad_keys, cosine, signed, far, head_size, own
    )
    keep("attn kept", (hidden_a, grad_qkv, grad_mix, attn_low), "r1")

    def attn_grads():
        hidden_a, grad_qkv, grad_mix, attn_low = got["attn kept"]
        return [over_tokens(hidden_a, grad_qkv), over_tokens(grad_mix, attn_low)]

    plan_grad("attn grads", attn_grads, *G_GRAD_ATTN)
    grad_normed_a = scatter_rows(
        ("r0", "r1", "r2"), [dot_last(g, qkv_full).astype(LOW) for g in grad_qkv]
    )
    grad_in = (grad_middle + norm_back(grad_normed_a, normed_a, inv_a)).astype(LOW)

    (grad_in,) = gate("in", [grad_in])
    in_rows = every_row(grad_in)
    in_rows = gate("end", in_rows)
    out_rows = every_row((middle + got["out", "far"]).astype(LOW))
    grad_gate, grad_up, grad_down, mlp_terms = finish_weights(
        scalars, got["mlp grads"], [gate_weight, up_weight], gain_b
    )
    grad_query_w, grad_key_w, grad_value_w, grad_proj, attn_terms = finish_weights(
        scalars, got["attn grads"], [query_weight, key_weight, value_weight], gain_a
    )
    layer_out = place_wide(scalars, out_rows, head_spots, tok, width, LOW)
    input_grad = place_wide(scalars, in_rows, head_spots, tok, width)
    terms = head_sum(jnp.concatenate([attn_terms, mlp_terms], axis=1).T)
    return (
        layer_out,
        input_grad,
        grad_query_w,
        grad_key_w,
        grad_value_w,
        grad_proj,
        grad_gate,
        grad_up,
        grad_down,
        terms[0],
        terms[1],
    )


def solution(mesh):
    return jax.shard_map(
        local,
        mesh=mesh,
        in_specs=(
            P("seq", None),
            P("seq", None),
            P(),
            P("seq"),
            P("seq", "head"),
            P("seq", "head"),
            P("seq", "head"),
            P("head", "seq"),
            P("seq"),
            P("seq", "head"),
            P("seq", "head"),
            P("head", "seq"),
        ),
        out_specs=(
            P("seq", None),
            P("seq", None),
            P("seq", "head"),
            P("seq", "head"),
            P("seq", "head"),
            P("head", "seq"),
            P("seq", "head"),
            P("seq", "head"),
            P("head", "seq"),
            P("seq"),
            P("seq"),
        ),
        check_vma=False,
    )
```

```python
import functools
import math

import jax
import jax.numpy as jnp
from jax import lax
from jax.experimental import pallas as pl
from jax.experimental.pallas import tpu as pltpu
from jax.sharding import PartitionSpec as P

HD = 128
EPSILON = 1e-05
ROPE_BASE = 10000.0
LOG_BIAS = math.log(4096.0)
LOW = jnp.bfloat16
F32 = jnp.float32
G_ATTN = (("start", "x1"), [("x1", "x2")])
G_TOP = (("z1n", "z2n"), ("z2n", "h0"), ("z2n", "h1"))
G_MLP = (("x1", "z1"), [("z1", "z2n"), ("z2n", "h1")])
G_GRAD_MLP = (("g2", "m2"), ("back", "r2"))
G_OUT = (("m0", "m1"), ("m1", "kvb"), ("m2", "kvb"), ("r2n", "end"))
G_GRAD_ATTN = (("r1n", "r2n"), ("r2n", "end"))
VMEM_ASK = 40 * 1024 * 1024


def dot(left_mat, right_mat):
    return lax.dot_general(
        left_mat, right_mat, (((1,), (0,)), ((), ())), preferred_element_type=F32
    )


def dot_last(left_mat, right_mat):
    return lax.dot_general(
        left_mat, right_mat, (((1,), (1,)), ((), ())), preferred_element_type=F32
    )


def dot_first(left_mat, right_mat):
    return lax.dot_general(
        left_mat, right_mat, (((0,), (0,)), ((), ())), preferred_element_type=F32
    )


def inv_rms(values):
    return lax.rsqrt(jnp.mean(values * values, axis=-1, keepdims=True) + EPSILON)


def norm_back(grad_normed, normed, inv_root):
    return inv_root * (
        grad_normed - normed * jnp.mean(grad_normed * normed, axis=-1, keepdims=True)
    )


def pick(stacked, index):
    return lax.dynamic_index_in_dim(stacked, index, 0, keepdims=False)


class Flow:
    def __init__(self):
        self.plans, self.got, self.due = {}, {}, {}

    def plan(self, name, start, end, make, send):
        self.plans.setdefault(start, []).append((name, end, make, send))

    def gate(self, label, values):
        planned = self.plans.pop(label, [])
        names = self.due.pop(label, [])
        ended = [self.got[name] for name in names]
        values, ended, operands = lax.optimization_barrier(
            (list(values), ended, [make() for _, _, make, _ in planned])
        )
        self.got.update(zip(names, ended))
        for (name, end, _, send), operand in zip(planned, operands):
            self.got[name] = send(operand)
            self.due.setdefault(end, []).append(name)
        return values


def shape_of(rows, cols, kind):
    return jax.ShapeDtypeStruct((rows, cols), kind)


def at_rows(index, count):
    return pl.ds(pl.multiple_of(index * count, count), count)


SMEM_SPEC = pl.BlockSpec(memory_space=pltpu.SMEM)
ANY_SPEC = pl.BlockSpec(memory_space=pl.ANY)
VMEM_SPEC = pl.BlockSpec(memory_space=pltpu.VMEM)


def call(body, outs, scalars, arrays, scratch=(), space=VMEM_SPEC, flops=0):
    outs = tuple(outs)
    moved = sum(math.prod(a.shape) * a.dtype.itemsize for a in tuple(arrays) + outs)
    return pl.pallas_call(
        body,
        out_shape=outs,
        in_specs=[SMEM_SPEC] + [space] * len(arrays),
        out_specs=tuple([space] * len(outs)),
        scratch_shapes=list(scratch),
        compiler_params=pltpu.CompilerParams(vmem_limit_bytes=VMEM_ASK),
        cost_estimate=pl.CostEstimate(flops=flops, bytes_accessed=moved, transcendentals=0),
    )(scalars, *arrays)


def place(scalars, entries, rows, height, breadth):
    number = len(entries)
    blocks = entries[0][0].shape[0] // height

    def body(at, *refs):
        ins, out, sems = refs[:number], refs[number], refs[number + 1]
        copies = []
        for n, (_, first, target, count, spot) in enumerate(entries):
            for i in range(blocks):
                copies.append(
                    pltpu.make_async_copy(
                        ins[n].at[i * height : (i + 1) * height, first : first + count],
                        out.at[at_rows(spot(at, i), height), target : target + count],
                        sems.at[n * blocks + i],
                    )
                )
        for copy in copies:
            copy.start()
        for copy in copies:
            copy.wait()

    return call(
        body,
        [shape_of(rows, breadth, LOW)],
        scalars,
        [entry[0] for entry in entries],
        [pltpu.SemaphoreType.DMA((number * blocks,))],
        ANY_SPEC,
    )[0]


def place_wide(scalars, pieces, spots, rows, cols, kind=F32):
    count = len(pieces)

    def body(at, *refs):
        out = refs[count]
        for n in range(count):
            out[at_rows(spots[n](at), pieces[n].shape[0]), :] = refs[n][...].astype(kind)

    return call(body, [shape_of(rows, cols, kind)], scalars, pieces)[0]


def finish_weights(scalars, pieces, weights, gain):
    many = len(weights)
    height, breadth = weights[0].shape
    count, block = pieces.shape[0], pieces.shape[2] // (many + 1)

    def body(at, piece_ref, *refs):
        held, gains = refs[:many], refs[many]
        outs, turned, terms = refs[many + 1 : -2], refs[-2], refs[-1]
        total = jnp.zeros((height, 1), F32)
        scale = gains[...]
        for i in range(count):
            where = slice(i * block, (i + 1) * block)
            for m in range(many):
                grad = piece_ref[i, :, m * block : (m + 1) * block].astype(F32)
                outs[m][:, where] = grad * scale
                total += jnp.sum(grad * held[m][:, where].astype(F32), axis=1, keepdims=True)
            turned[where, :] = piece_ref[i, :, many * block :].astype(F32).T
        terms[...] = total

    outs = [shape_of(height, breadth, F32) for _ in weights]
    outs += [shape_of(breadth, height, F32), shape_of(height, 1, F32)]
    return call(body, outs, scalars, [pieces] + list(weights) + [gain])


def turn(values, cosine, signed):
    return values * cosine + pltpu.roll(values, HD // 2, 1) * signed


def piece_spots(far, head_size, own):
    for c in range(2):
        row = 0
        for first in (0, far // 2):
            for y in range(head_size // 2):
                for k in range(first, first + far // 2):
                    yield c, row, k, 2 * y + c
                    row += own


def rotate_all(scalars, chunks, cosine, signed, far, head_size, own):
    tok = own * head_size

    def body(at, low_ref, high_ref, cos_ref, sin_ref, query_ref, kv_ref):
        ins = (low_ref, high_ref)
        for c, row, k, m in piece_spots(far, head_size, own):
            spot = pl.ds(
                pl.multiple_of((at[0] ^ k) * tok + (at[1] ^ m) * own, own), own
            )
            cos_rows, sin_rows = cos_ref[spot, :], sin_ref[spot, :]
            value = ins[c][row : row + own, :]
            query_ref[spot, :] = turn(value[:, :HD], cos_rows, sin_rows).astype(LOW)
            kv_ref[spot, :HD] = turn(value[:, HD : 2 * HD], cos_rows, sin_rows).astype(LOW)
            kv_ref[spot, HD:] = value[:, 2 * HD :].astype(LOW)

    rows = far * tok
    return call(
        body,
        [shape_of(rows, HD, LOW), shape_of(rows, 2 * HD, LOW)],
        scalars,
        list(chunks) + [cosine, signed],
    )


def live_pairs(at, groups, far, tok):
    for i in range(far):
        for g in range(groups):
            for j in range(i + 1):
                yield i, g, j


def probabilities(at, query, key, query_doc, key_doc, i, g, j, groups):
    scores = lax.dot_general(query, key, (((1,), (1,)), ((), ())), preferred_element_type=F32)
    live = query_doc == key_doc
    if i == j:
        if g == 0:
            rows = lax.broadcasted_iota(jnp.int32, scores.shape, 0)
            cols = lax.broadcasted_iota(jnp.int32, scores.shape, 1)
            live = live & (rows >= cols)
        else:
            source = lax.rem(at[2] - g + groups, groups)
            live = live & (query_doc >= jnp.where(source < at[2], 0, 1 << 30))
    return jnp.where(live, jax.nn.sigmoid(scores * HD**-0.5 - LOG_BIAS), 0.0)


def attend(scalars, query, keys, query_doc, key_doc, far, head_size, own):
    tok, groups = own * head_size, len(keys)

    def body(at, query_ref, doc_ref, key_doc_ref, *refs):
        key_refs, (low_ref, high_ref, held) = refs[:groups], refs[groups:]
        for i in range(far):
            block = query_ref[i * tok : (i + 1) * tok, :]
            docs = doc_ref[i * tok : (i + 1) * tok, :]
            total = jnp.zeros((tok, HD), F32)
            for j in range(i + 1):
                for g in range(groups):
                    span = slice(j * tok, (j + 1) * tok)
                    probs = probabilities(
                        at, block, key_refs[g][span, :HD], docs, key_doc_ref[g : g + 1, span], i, g, j, groups
                    )
                    total += dot(probs.astype(LOW), key_refs[g][span, HD:])
            held[i * tok : (i + 1) * tok, :] = total.astype(LOW)
        outs = (low_ref, high_ref)
        for c, row, k, m in piece_spots(far, head_size, own):
            spot = pl.ds(
                pl.multiple_of((at[0] ^ k) * tok + (at[1] ^ m) * own, own), own
            )
            outs[c][row : row + own, :] = held[spot, :]

    rows = far * tok
    return call(
        body,
        [shape_of(rows // 2, HD, LOW)] * 2,
        scalars,
        [query, query_doc, key_doc] + list(keys),
        [pltpu.VMEM((rows, HD), LOW)],
        flops=4 * rows * rows * groups * HD // 2,
    )


def attend_back(scalars, query, keys, query_doc, key_doc, grads, far, head_size, own):
    tok, groups = own * head_size, len(keys)

    def body(at, query_ref, doc_ref, key_doc_ref, low_ref, high_ref, *refs):
        key_refs, outs, held = refs[:groups], refs[groups:-1], refs[-1]
        query_out, key_outs = outs[0], outs[1:]
        ins = (low_ref, high_ref)
        for c, row, k, m in piece_spots(far, head_size, own):
            spot = pl.ds(
                pl.multiple_of((at[0] ^ k) * tok + (at[1] ^ m) * own, own), own
            )
            held[spot, :] = ins[c][row : row + own, :]
        for j in range(far):
            for g in range(groups):
                span = slice(j * tok, (j + 1) * tok)
                key, value = key_refs[g][span, :HD], key_refs[g][span, HD:]
                key_total = jnp.zeros((tok, HD), F32)
                value_total = jnp.zeros((tok, HD), F32)
                for i in range(j, far):
                    rows = slice(i * tok, (i + 1) * tok)
                    block, grad = query_ref[rows, :], held[rows, :]
                    probs = probabilities(
                        at, block, key, doc_ref[rows, :], key_doc_ref[g : g + 1, span], i, g, j, groups
                    )
                    value_total += dot_first(probs.astype(LOW), grad)
                    terms = (dot_last(grad, value) * probs * (1.0 - probs)).astype(LOW)
                    key_total += dot_first(terms, block)
                    part = dot(terms, key) * HD**-0.5
                    if j == 0 and g == 0:
                        query_out[rows, :] = part
                    else:
                        query_out[rows, :] += part
                kind = key_outs[g].dtype
                key_outs[g][span, :HD] = (key_total * HD**-0.5).astype(kind)
                key_outs[g][span, HD:] = value_total.astype(kind)

    rows = far * tok
    return call(
        body,
        [shape_of(rows, HD, F32), shape_of(rows, 2 * HD, F32)]
        + [shape_of(rows, 2 * HD, LOW)] * (groups - 1),
        scalars,
        [query, query_doc, key_doc] + list(grads) + list(keys),
        [pltpu.VMEM((rows, HD), LOW)],
        flops=10 * rows * rows * groups * HD // 2,
    )


def rotate_back(scalars, query, keys, cosine, signed, far, head_size, own):
    tok, count = own * head_size, len(keys)

    def body(at, query_ref, cos_ref, sin_ref, *refs):
        key_refs, outs = refs[:count], refs[count:]
        for c, row, k, m in piece_spots(far, head_size, own):
            spot = pl.ds(
                pl.multiple_of((at[0] ^ k) * tok + (at[1] ^ m) * own, own), own
            )
            cos_rows, sin_rows = cos_ref[spot, :], -sin_ref[spot, :]
            total = key_refs[0][spot, :]
            for ref in key_refs[1:]:
                total += ref[spot, :].astype(F32)
            rows = slice(row, row + own)
            outs[c][rows, :HD] = turn(query_ref[spot, :], cos_rows, sin_rows).astype(LOW)
            outs[c][rows, HD : 2 * HD] = turn(total[:, :HD], cos_rows, sin_rows).astype(LOW)
            outs[c][rows, 2 * HD :] = total[:, HD:].astype(LOW)

    rows = far * tok
    return call(
        body,
        [shape_of(rows // 2, 3 * HD, LOW)] * 2,
        scalars,
        [query, cosine, signed] + list(keys),
    )


def local(
    layer_in,
    out_grad,
    doc_ids,
    attn_gain,
    query_weight,
    key_weight,
    value_weight,
    proj_weight,
    mlp_gain,
    gate_weight,
    up_weight,
    down_weight,
):
    tok, width = layer_in.shape
    seq_size, head_size = lax.axis_size("seq"), lax.axis_size("head")
    far = query_weight.shape[1] // HD
    groups = seq_size // far
    own = tok // head_size
    seq_at, head_at = lax.axis_index("seq"), lax.axis_index("head")
    far_at, group_at = seq_at // groups, seq_at % groups
    scalars = jnp.stack([far_at, head_at, group_at]).astype(jnp.int32)
    rows_s = width // seq_size
    hidden = gate_weight.shape[1] // far
    tok_group = far * tok

    def far_swap(value, step):
        return lax.ppermute(
            value,
            "seq",
            [(i * groups + g, (i ^ step) * groups + g) for i in range(far) for g in range(groups)],
        )

    def gather_far(piece):
        return [piece] + [far_swap(piece, k) for k in range(1, far)]

    def scatter_far(parts):
        total = parts[0].astype(F32)
        for k in reversed(range(1, far)):
            total = total + far_swap(parts[k].astype(LOW), k).astype(F32)
        return total

    def far_exchange(blocks):
        return lax.all_to_all(
            blocks,
            "seq",
            0,
            0,
            axis_index_groups=[[i * groups + g for i in range(far)] for g in range(groups)],
            tiled=True,
        )

    def group_shift(value, step):
        return lax.ppermute(
            value,
            "seq",
            [
                (i * groups + g, i * groups + (g + step) % groups)
                for i in range(far)
                for g in range(groups)
            ],
        )

    def head_swap(value, step):
        return lax.ppermute(value, "head", [(i, i ^ step) for i in range(head_size)])

    flow = Flow()
    gate, plan, got = flow.gate, flow.plan, flow.got

    def keep(name, value, label):
        got[name] = value
        flow.due.setdefault(label, []).append(name)
    half_far = far // 2
    many_rows = half_far * own

    def core_swap(value):
        parts = [value[i : i + own] for i in range(0, value.shape[0], own)]
        return jnp.concatenate([head_swap(part, 1) for part in parts])

    def gather_rows(labels, piece):
        (piece,) = gate(labels[0], [piece])
        parts = gather_far(piece)
        near = jnp.concatenate(
            parts[:half_far] + [head_swap(part, 2) for part in parts[:half_far]]
        )
        (near,) = gate(labels[0] + "n", [near])
        rest = jnp.concatenate(parts[half_far:])
        near, rest = gate(labels[1], [near, rest])
        rest = jnp.concatenate([rest, head_swap(rest, 2)])
        near_got = core_swap(near)
        near, rest, near_got = gate(labels[2], [near, rest, near_got])
        return [
            jnp.concatenate([near, rest]),
            jnp.concatenate([near_got, core_swap(rest)]),
        ]

    def split_rows(chunks):
        return [[c[: 2 * many_rows], c[2 * many_rows :]] for c in chunks]

    def scatter_rows(labels, chunks):
        mine, other = split_rows(chunks)
        *mine, other[0], other[1] = gate(labels[0], mine + other)
        half = mine[1].astype(F32) + core_swap(other[1]).astype(F32)
        kept, sent, *left = gate(
            labels[1], [half[:many_rows], half[many_rows:].astype(LOW), mine[0], other[0]]
        )
        near = left[0].astype(F32) + core_swap(left[1]).astype(F32)
        (near,) = gate(labels[1] + "n", [near])
        rest = kept + head_swap(sent, 2).astype(F32)
        near, near_sent, rest = gate(
            labels[2], [near[:many_rows], near[many_rows:].astype(LOW), rest]
        )
        near = near + head_swap(near_sent, 2).astype(F32)
        (near,) = gate(labels[2] + "n", [near])
        return scatter_far(
            [part[k * own : (k + 1) * own] for part in (near, rest) for k in range(half_far)]
        )

    def plan_gather(tag, piece, far_gates, near_gates, rest_gates):
        plan((tag, "far"), *far_gates, lambda: piece, gather_far)
        halves = (("near", range(half_far), near_gates), ("rest", range(half_far, far), rest_gates))
        for name, ks, gates in halves:
            plan(
                (tag, name),
                *gates,
                lambda ks=ks: jnp.concatenate([got[tag, "far"][k] for k in ks]),
                lambda v: head_swap(v, 2),
            )

        def finish():
            parts = got[tag, "far"]
            mine = parts[:half_far] + [got[tag, "near"]] + parts[half_far:] + [got[tag, "rest"]]
            mine = jnp.concatenate(mine)
            return [mine, core_swap(mine)]

        return finish

    def plan_scatter(tag, chunks, core_gates, rest_gates, near_gates, far_gates):
        made = []

        def halves():
            if not made:
                made.extend(split_rows(chunks()))
            return made

        def half(n):
            mine = halves()[0]
            return mine[n].astype(F32) + got[tag, "core", n].astype(F32)

        def part(k):
            n, at = k // half_far, k % half_far * own
            value = half(n)[:many_rows] + got[tag, "head", n].astype(F32)
            return value[at : at + own].astype(LOW)

        for n, gates in ((1, rest_gates), (0, near_gates)):
            plan((tag, "core", n), *core_gates, lambda n=n: halves()[1][n], core_swap)
            plan(
                (tag, "head", n),
                *gates,
                lambda n=n: half(n)[many_rows:].astype(LOW),
                lambda v: head_swap(v, 2),
            )
        plan(
            (tag, "far"),
            *far_gates,
            lambda: jnp.stack([part(k) for k in range(far)]),
            lambda v: scatter_far([v[k] for k in range(far)]),
        )

    def column_blocks(weight, gain=None):
        breadth = weight.shape[1] // far
        blocks = [weight[:, i * breadth : (i + 1) * breadth] for i in range(far)]
        if gain is not None:
            blocks = [(block.astype(F32) * gain).astype(LOW) for block in blocks]
        return jnp.stack(blocks)

    def row_blocks(weight):
        return weight.reshape(far, weight.shape[0] // far, weight.shape[1]).transpose(0, 2, 1)

    def plan_weight(name, make, breadth, far_gates, group_gates):
        plan(name, *far_gates, make, far_exchange)
        step = breadth // len(group_gates)
        for n, gates in enumerate(group_gates):
            for g in range(1, groups):
                plan(
                    (name, n, g),
                    *gates,
                    lambda n=n: got[name][:, :, n * step : (n + 1) * step],
                    lambda v, g=g: group_shift(v, g),
                )

    def place_weight(name, first, breadth):
        def flat(value):
            return value.reshape(-1, value.shape[2])

        def spot(g):
            return lambda at, i: i * groups + lax.rem(at[2] + groups - g, groups)

        entries = [(flat(got[name]), first, 0, breadth, spot(0))]
        for g in range(1, groups):
            n, start = 0, 0
            while (name, n, g) in got:
                piece = flat(got[name, n, g])
                stop = start + piece.shape[1]
                begin, end = max(first, start), min(first + breadth, stop)
                if begin < end:
                    entries.append((piece, begin - start, begin - first, end - begin, spot(g)))
                n, start = n + 1, stop
        return place(scalars, entries, width, rows_s, breadth)

    def plan_grad(name, make, group_gates, far_gates):
        made = []

        def part(at):
            if not made:
                made.extend(v.reshape(far, groups, rows_s, -1) for v in make())
            return jnp.concatenate(
                [lax.dynamic_index_in_dim(v, at, 1, keepdims=False) for v in made], axis=2
            )

        def total():
            value = part(group_at)
            for g in range(1, groups):
                value = value + got[name, "group", g].astype(F32)
            return value.astype(LOW)

        for g in range(1, groups):
            plan(
                (name, "group", g),
                *group_gates,
                lambda g=g: part((group_at + g) % groups).astype(LOW),
                lambda v, g=g: group_shift(v, g),
            )
        plan(name, *far_gates, total, far_exchange)

    head_spots = [(lambda at, m=m: at[1] ^ m) for m in (0, 2, 1, 3)]

    def every_row(piece):
        half = [piece, head_swap(piece, 2)]
        return half + [head_swap(part, 1) for part in half]

    def head_sum(value):
        value = value + head_swap(value, 1)
        return value + head_swap(value, 2)

    gain_a = attn_gain.astype(F32)[:, None]
    gain_b = mlp_gain.astype(F32)[:, None]

    own_in = lax.dynamic_slice_in_dim(layer_in, head_at * own, own, 0).astype(F32)
    own_grad = lax.dynamic_slice_in_dim(out_grad, head_at * own, own, 0)
    inv_a = inv_rms(own_in)
    normed_a = own_in * inv_a
    plan_weight(
        "attn",
        lambda: jnp.concatenate(
            [column_blocks(w, gain_a) for w in (query_weight, key_weight, value_weight)]
            + [row_blocks(proj_weight)],
            axis=2,
        ),
        4 * HD,
        *G_ATTN,
    )
    plan_weight(
        "mlp",
        lambda: jnp.concatenate(
            [column_blocks(w, gain_b) for w in (gate_weight, up_weight)] + [row_blocks(down_weight)],
            axis=2,
        ),
        3 * hidden,
        *G_MLP,
    )
    finish_top = plan_gather("top", own_grad, *G_TOP)
    gate("start", [])
    far_ids = jnp.arange(far, dtype=jnp.int32)
    positions = (far_ids * groups + group_at)[:, None] * tok + jnp.arange(tok, dtype=jnp.int32)
    frequency = ROPE_BASE ** (-jnp.arange(HD // 2, dtype=F32) * 2.0 / HD)
    angles = positions.reshape(tok_group).astype(F32)[:, None] * frequency[None, :]
    cosine, sine_tab = jnp.cos(angles), jnp.sin(angles)
    cosine = jnp.concatenate([cosine, cosine], axis=1)
    signed = jnp.concatenate([-sine_tab, sine_tab], axis=1)
    docs = doc_ids.reshape(far, groups, tok)
    query_doc = lax.dynamic_index_in_dim(docs, group_at, 1, keepdims=False).reshape(tok_group, 1)
    key_doc = jnp.stack(
        [
            lax.dynamic_index_in_dim(docs, (group_at - g) % groups, 1, keepdims=False).reshape(
                tok_group
            )
            for g in range(groups)
        ]
    )
    keep("tables", (cosine, signed, query_doc, key_doc), "x0n")
    hidden_a = gather_rows(("x0", "x1", "x2"), normed_a.astype(LOW))
    qkv_full, proj_turned = place_weight("attn", 0, 3 * HD), place_weight("attn", 3 * HD, HD)

    cosine, signed, query_doc, key_doc = got["tables"]
    hidden_a = gate("qkv", hidden_a)
    query_rot, key_own = rotate_all(
        scalars, [dot(h, qkv_full) for h in hidden_a], cosine, signed, far, head_size, own
    )
    key_own, query_rot = gate("kv", [key_own, query_rot])
    keys = [key_own] + [group_shift(key_own, g) for g in range(1, groups)]

    query_rot, *keys = gate("attend", [query_rot] + keys)
    attn_low = attend(scalars, query_rot, keys, query_doc, key_doc, far, head_size, own)
    middle = own_in + scatter_rows(("z0", "z1", "z2"), [dot_last(a, proj_turned).astype(LOW) for a in attn_low])

    inv_b = inv_rms(middle)
    normed_b = middle * inv_b
    hidden_b = gather_rows(("h0", "h1", "h2"), normed_b.astype(LOW))
    hidden_b = gate("mlp", hidden_b)
    gate_up = place_weight("mlp", 0, 2 * hidden)
    down_turned = place_weight("mlp", 2 * hidden, hidden)
    parts, active = [], []
    for h in hidden_b:
        gate_up_val = dot(h, gate_up)
        gate_val, up_val = gate_up_val[:, :hidden], gate_up_val[:, hidden:]
        gate_sig = jax.nn.sigmoid(gate_val)
        silu_val = gate_val * gate_sig
        active.append((silu_val * up_val).astype(LOW))
        parts.append(
            (silu_val, up_val * gate_sig * (1.0 + gate_val * (1.0 - gate_sig)))
        )
    plan_scatter(
        "out", lambda: [dot_last(a, down_turned).astype(LOW) for a in active], *G_OUT
    )
    grad_top = finish_top()
    grad_gu = []
    for top, (silu_val, gate_slope) in zip(grad_top, parts):
        grad_active = dot(top, down_turned)
        grad_gu.append(
            jnp.concatenate(
                [(grad_active * gate_slope).astype(LOW), (grad_active * silu_val).astype(LOW)],
                axis=1,
            )
        )

    def over_tokens(left_mats, right_mats):
        return sum(dot_first(a, b) for a, b in zip(left_mats, right_mats))

    keep("mlp kept", (hidden_b, grad_gu, grad_top, active), "g1n")

    def mlp_grads():
        hidden_b, grad_gu, grad_top, active = got["mlp kept"]
        return [over_tokens(hidden_b, grad_gu), over_tokens(grad_top, active)]

    plan_grad("mlp grads", mlp_grads, *G_GRAD_MLP)
    grad_normed_b = scatter_rows(
        ("g0", "g1", "g2"),
        [
            dot_last(g, gate_up).astype(LOW) for g in grad_gu
        ],
    )
    grad_middle = own_grad.astype(F32) + norm_back(grad_normed_b, normed_b, inv_b)
    grad_mix = gather_rows(("m0", "m1", "m2"), grad_middle.astype(LOW))

    grad_mix = gate("back", grad_mix)
    grad_attn = [dot(g, proj_turned).astype(LOW) for g in grad_mix]
    grad_query, *grad_keys = attend_back(
        scalars, query_rot, keys, query_doc, key_doc, grad_attn, far, head_size, own
    )
    grad_query, *grad_keys = gate("kvb", [grad_query] + grad_keys)
    grad_keys = [grad_keys[0]] + [
        group_shift(grad_keys[g], groups - g) for g in range(1, groups)
    ]
    grad_query, *grad_keys = gate("turn", [grad_query] + grad_keys)
    grad_qkv = rotate_back(
        scalars, grad_query, grad_keys, cosine, signed, far, head_size, own
    )
    keep("attn kept", (hidden_a, grad_qkv, grad_mix, attn_low), "r1")

    def attn_grads():
        hidden_a, grad_qkv, grad_mix, attn_low = got["attn kept"]
        return [over_tokens(hidden_a, grad_qkv), over_tokens(grad_mix, attn_low)]

    plan_grad("attn grads", attn_grads, *G_GRAD_ATTN)
    grad_normed_a = scatter_rows(
        ("r0", "r1", "r2"), [dot_last(g, qkv_full).astype(LOW) for g in grad_qkv]
    )
    grad_in = (grad_middle + norm_back(grad_normed_a, normed_a, inv_a)).astype(LOW)

    (grad_in,) = gate("in", [grad_in])
    in_rows = every_row(grad_in)
    in_rows = gate("end", in_rows)
    out_rows = every_row((middle + got["out", "far"]).astype(LOW))
    grad_gate, grad_up, grad_down, mlp_terms = finish_weights(
        scalars, got["mlp grads"], [gate_weight, up_weight], gain_b
    )
    grad_query_w, grad_key_w, grad_value_w, grad_proj, attn_terms = finish_weights(
        scalars, got["attn grads"], [query_weight, key_weight, value_weight], gain_a
    )
    layer_out = place_wide(scalars, out_rows, head_spots, tok, width, LOW)
    input_grad = place_wide(scalars, in_rows, head_spots, tok, width)
    terms = head_sum(jnp.concatenate([attn_terms, mlp_terms], axis=1).T)
    return (
        layer_out,
        input_grad,
        grad_query_w,
        grad_key_w,
        grad_value_w,
        grad_proj,
        grad_gate,
        grad_up,
        grad_down,
        terms[0],
        terms[1],
    )


def solution(mesh):
    return jax.shard_map(
        local,
        mesh=mesh,
        in_specs=(
            P("seq", None),
            P("seq", None),
            P(),
            P("seq"),
            P("seq", "head"),
            P("seq", "head"),
            P("seq", "head"),
            P("head", "seq"),
            P("seq"),
            P("seq", "head"),
            P("seq", "head"),
            P("head", "seq"),
        ),
        out_specs=(
            P("seq", None),
            P("seq", None),
            P("seq", "head"),
            P("seq", "head"),
            P("seq", "head"),
            P("head", "seq"),
            P("seq", "head"),
            P("seq", "head"),
            P("head", "seq"),
            P("seq"),
            P("seq"),
        ),
        check_vma=False,
    )
```

```python
import functools
import math

import jax
import jax.numpy as jnp
from jax import lax
from jax.experimental import pallas as pl
from jax.experimental.pallas import tpu as pltpu
from jax.sharding import PartitionSpec as P

HD = 128
EPSILON = 1e-05
ROPE_BASE = 10000.0
LOG_BIAS = math.log(4096.0)
LOW = jnp.bfloat16
F32 = jnp.float32
G_ATTN = (("start", "x1"), [("x1", "x2")])
G_TOP = (("z1n", "z2n"), ("z2n", "h0"), ("z2n", "h1"))
G_MLP = (("x1", "z1"), [("z1", "z2n"), ("z2n", "h1")])
G_GRAD_MLP = (("g2", "m2"), ("back", "r2n"))
G_OUT = (("m0", "m1"), ("m1", "kvb"), ("m2", "kvb"), ("r2n", "end"))
G_GRAD_ATTN = (("r1n", "r2n"), ("r2n", "end"))
VMEM_ASK = 40 * 1024 * 1024


def dot(left_mat, right_mat):
    return lax.dot_general(
        left_mat, right_mat, (((1,), (0,)), ((), ())), preferred_element_type=F32
    )


def dot_last(left_mat, right_mat):
    return lax.dot_general(
        left_mat, right_mat, (((1,), (1,)), ((), ())), preferred_element_type=F32
    )


def dot_first(left_mat, right_mat):
    return lax.dot_general(
        left_mat, right_mat, (((0,), (0,)), ((), ())), preferred_element_type=F32
    )


def inv_rms(values):
    return lax.rsqrt(jnp.mean(values * values, axis=-1, keepdims=True) + EPSILON)


def norm_back(grad_normed, normed, inv_root):
    return inv_root * (
        grad_normed - normed * jnp.mean(grad_normed * normed, axis=-1, keepdims=True)
    )


def pick(stacked, index):
    return lax.dynamic_index_in_dim(stacked, index, 0, keepdims=False)


class Flow:
    def __init__(self):
        self.plans, self.got, self.due = {}, {}, {}

    def plan(self, name, start, end, make, send):
        self.plans.setdefault(start, []).append((name, end, make, send))

    def gate(self, label, values):
        planned = self.plans.pop(label, [])
        names = self.due.pop(label, [])
        ended = [self.got[name] for name in names]
        values, ended, operands = lax.optimization_barrier(
            (list(values), ended, [make() for _, _, make, _ in planned])
        )
        self.got.update(zip(names, ended))
        for (name, end, _, send), operand in zip(planned, operands):
            self.got[name] = send(operand)
            self.due.setdefault(end, []).append(name)
        return values


def shape_of(rows, cols, kind):
    return jax.ShapeDtypeStruct((rows, cols), kind)


def at_rows(index, count):
    return pl.ds(pl.multiple_of(index * count, count), count)


SMEM_SPEC = pl.BlockSpec(memory_space=pltpu.SMEM)
ANY_SPEC = pl.BlockSpec(memory_space=pl.ANY)
VMEM_SPEC = pl.BlockSpec(memory_space=pltpu.VMEM)


def call(body, outs, scalars, arrays, scratch=(), space=VMEM_SPEC, flops=0):
    outs = tuple(outs)
    moved = sum(math.prod(a.shape) * a.dtype.itemsize for a in tuple(arrays) + outs)
    return pl.pallas_call(
        body,
        out_shape=outs,
        in_specs=[SMEM_SPEC] + [space] * len(arrays),
        out_specs=tuple([space] * len(outs)),
        scratch_shapes=list(scratch),
        compiler_params=pltpu.CompilerParams(vmem_limit_bytes=VMEM_ASK),
        cost_estimate=pl.CostEstimate(flops=flops, bytes_accessed=moved, transcendentals=0),
    )(scalars, *arrays)


def place(scalars, entries, rows, height, breadth):
    number = len(entries)
    blocks = entries[0][0].shape[0] // height

    def body(at, *refs):
        ins, out, sems = refs[:number], refs[number], refs[number + 1]
        copies = []
        for n, (_, first, target, count, spot) in enumerate(entries):
            for i in range(blocks):
                copies.append(
                    pltpu.make_async_copy(
                        ins[n].at[i * height : (i + 1) * height, first : first + count],
                        out.at[at_rows(spot(at, i), height), target : target + count],
                        sems.at[n * blocks + i],
                    )
                )
        for copy in copies:
            copy.start()
        for copy in copies:
            copy.wait()

    return call(
        body,
        [shape_of(rows, breadth, LOW)],
        scalars,
        [entry[0] for entry in entries],
        [pltpu.SemaphoreType.DMA((number * blocks,))],
        ANY_SPEC,
    )[0]


def place_wide(scalars, pieces, spots, rows, cols, kind=F32):
    count = len(pieces)

    def body(at, *refs):
        out = refs[count]
        for n in range(count):
            out[at_rows(spots[n](at), pieces[n].shape[0]), :] = refs[n][...].astype(kind)

    return call(body, [shape_of(rows, cols, kind)], scalars, pieces)[0]


def finish_weights(scalars, pieces, weights, gain):
    many = len(weights)
    height, breadth = weights[0].shape
    count, block = pieces.shape[0], pieces.shape[2] // (many + 1)

    def body(at, piece_ref, *refs):
        held, gains = refs[:many], refs[many]
        outs, turned, terms = refs[many + 1 : -2], refs[-2], refs[-1]
        total = jnp.zeros((height, 1), F32)
        scale = gains[...]
        for i in range(count):
            where = slice(i * block, (i + 1) * block)
            for m in range(many):
                grad = piece_ref[i, :, m * block : (m + 1) * block].astype(F32)
                outs[m][:, where] = grad * scale
                total += jnp.sum(grad * held[m][:, where].astype(F32), axis=1, keepdims=True)
            turned[where, :] = piece_ref[i, :, many * block :].astype(F32).T
        terms[...] = total

    outs = [shape_of(height, breadth, F32) for _ in weights]
    outs += [shape_of(breadth, height, F32), shape_of(height, 1, F32)]
    return call(body, outs, scalars, [pieces] + list(weights) + [gain])


def turn(values, cosine, signed):
    return values * cosine + pltpu.roll(values, HD // 2, 1) * signed


def piece_spots(far, head_size, own):
    for c in range(2):
        row = 0
        for first in (0, far // 2):
            for y in range(head_size // 2):
                for k in range(first, first + far // 2):
                    yield c, row, k, 2 * y + c
                    row += own


def rotate_all(scalars, chunks, cosine, signed, far, head_size, own):
    tok = own * head_size

    def body(at, low_ref, high_ref, cos_ref, sin_ref, query_ref, kv_ref):
        ins = (low_ref, high_ref)
        for c, row, k, m in piece_spots(far, head_size, own):
            spot = pl.ds(
                pl.multiple_of((at[0] ^ k) * tok + (at[1] ^ m) * own, own), own
            )
            cos_rows, sin_rows = cos_ref[spot, :], sin_ref[spot, :]
            value = ins[c][row : row + own, :]
            query_ref[spot, :] = turn(value[:, :HD], cos_rows, sin_rows).astype(LOW)
            kv_ref[spot, :HD] = turn(value[:, HD : 2 * HD], cos_rows, sin_rows).astype(LOW)
            kv_ref[spot, HD:] = value[:, 2 * HD :].astype(LOW)

    rows = far * tok
    return call(
        body,
        [shape_of(rows, HD, LOW), shape_of(rows, 2 * HD, LOW)],
        scalars,
        list(chunks) + [cosine, signed],
    )


def live_pairs(at, groups, far, tok):
    for i in range(far):
        for g in range(groups):
            for j in range(i + 1):
                yield i, g, j


def probabilities(at, query, key, query_doc, key_doc, i, g, j, groups):
    scores = lax.dot_general(query, key, (((1,), (1,)), ((), ())), preferred_element_type=F32)
    live = query_doc == key_doc
    if i == j:
        if g == 0:
            rows = lax.broadcasted_iota(jnp.int32, scores.shape, 0)
            cols = lax.broadcasted_iota(jnp.int32, scores.shape, 1)
            live = live & (rows >= cols)
        else:
            source = lax.rem(at[2] - g + groups, groups)
            live = live & (query_doc >= jnp.where(source < at[2], 0, 1 << 30))
    return jnp.where(live, jax.nn.sigmoid(scores * HD**-0.5 - LOG_BIAS), 0.0)


def attend(scalars, query, keys, query_doc, key_doc, far, head_size, own):
    tok, groups = own * head_size, len(keys)

    def body(at, query_ref, doc_ref, key_doc_ref, *refs):
        key_refs, (low_ref, high_ref, held) = refs[:groups], refs[groups:]
        for i in range(far):
            block = query_ref[i * tok : (i + 1) * tok, :]
            docs = doc_ref[i * tok : (i + 1) * tok, :]
            total = jnp.zeros((tok, HD), F32)
            for j in range(i + 1):
                for g in range(groups):
                    span = slice(j * tok, (j + 1) * tok)
                    probs = probabilities(
                        at, block, key_refs[g][span, :HD], docs, key_doc_ref[g : g + 1, span], i, g, j, groups
                    )
                    total += dot(probs.astype(LOW), key_refs[g][span, HD:])
            held[i * tok : (i + 1) * tok, :] = total.astype(LOW)
        outs = (low_ref, high_ref)
        for c, row, k, m in piece_spots(far, head_size, own):
            spot = pl.ds(
                pl.multiple_of((at[0] ^ k) * tok + (at[1] ^ m) * own, own), own
            )
            outs[c][row : row + own, :] = held[spot, :]

    rows = far * tok
    return call(
        body,
        [shape_of(rows // 2, HD, LOW)] * 2,
        scalars,
        [query, query_doc, key_doc] + list(keys),
        [pltpu.VMEM((rows, HD), LOW)],
        flops=4 * rows * rows * groups * HD // 2,
    )


def attend_back(scalars, query, keys, query_doc, key_doc, grads, far, head_size, own):
    tok, groups = own * head_size, len(keys)

    def body(at, query_ref, doc_ref, key_doc_ref, low_ref, high_ref, *refs):
        key_refs, outs, held = refs[:groups], refs[groups:-1], refs[-1]
        query_out, key_outs = outs[0], outs[1:]
        ins = (low_ref, high_ref)
        for c, row, k, m in piece_spots(far, head_size, own):
            spot = pl.ds(
                pl.multiple_of((at[0] ^ k) * tok + (at[1] ^ m) * own, own), own
            )
            held[spot, :] = ins[c][row : row + own, :]
        for j in range(far):
            for g in range(groups):
                span = slice(j * tok, (j + 1) * tok)
                key, value = key_refs[g][span, :HD], key_refs[g][span, HD:]
                key_total = jnp.zeros((tok, HD), F32)
                value_total = jnp.zeros((tok, HD), F32)
                for i in range(j, far):
                    rows = slice(i * tok, (i + 1) * tok)
                    block, grad = query_ref[rows, :], held[rows, :]
                    probs = probabilities(
                        at, block, key, doc_ref[rows, :], key_doc_ref[g : g + 1, span], i, g, j, groups
                    )
                    value_total += dot_first(probs.astype(LOW), grad)
                    terms = (dot_last(grad, value) * probs * (1.0 - probs)).astype(LOW)
                    key_total += dot_first(terms, block)
                    part = dot(terms, key) * HD**-0.5
                    if j == 0 and g == 0:
                        query_out[rows, :] = part
                    else:
                        query_out[rows, :] += part
                kind = key_outs[g].dtype
                key_outs[g][span, :HD] = (key_total * HD**-0.5).astype(kind)
                key_outs[g][span, HD:] = value_total.astype(kind)

    rows = far * tok
    return call(
        body,
        [shape_of(rows, HD, F32), shape_of(rows, 2 * HD, F32)]
        + [shape_of(rows, 2 * HD, LOW)] * (groups - 1),
        scalars,
        [query, query_doc, key_doc] + list(grads) + list(keys),
        [pltpu.VMEM((rows, HD), LOW)],
        flops=10 * rows * rows * groups * HD // 2,
    )


def rotate_back(scalars, query, keys, cosine, signed, far, head_size, own):
    tok, count = own * head_size, len(keys)

    def body(at, query_ref, cos_ref, sin_ref, *refs):
        key_refs, outs = refs[:count], refs[count:]
        for c, row, k, m in piece_spots(far, head_size, own):
            spot = pl.ds(
                pl.multiple_of((at[0] ^ k) * tok + (at[1] ^ m) * own, own), own
            )
            cos_rows, sin_rows = cos_ref[spot, :], -sin_ref[spot, :]
            total = key_refs[0][spot, :]
            for ref in key_refs[1:]:
                total += ref[spot, :].astype(F32)
            rows = slice(row, row + own)
            outs[c][rows, :HD] = turn(query_ref[spot, :], cos_rows, sin_rows).astype(LOW)
            outs[c][rows, HD : 2 * HD] = turn(total[:, :HD], cos_rows, sin_rows).astype(LOW)
            outs[c][rows, 2 * HD :] = total[:, HD:].astype(LOW)

    rows = far * tok
    return call(
        body,
        [shape_of(rows // 2, 3 * HD, LOW)] * 2,
        scalars,
        [query, cosine, signed] + list(keys),
    )


def local(
    layer_in,
    out_grad,
    doc_ids,
    attn_gain,
    query_weight,
    key_weight,
    value_weight,
    proj_weight,
    mlp_gain,
    gate_weight,
    up_weight,
    down_weight,
):
    tok, width = layer_in.shape
    seq_size, head_size = lax.axis_size("seq"), lax.axis_size("head")
    far = query_weight.shape[1] // HD
    groups = seq_size // far
    own = tok // head_size
    seq_at, head_at = lax.axis_index("seq"), lax.axis_index("head")
    far_at, group_at = seq_at // groups, seq_at % groups
    scalars = jnp.stack([far_at, head_at, group_at]).astype(jnp.int32)
    rows_s = width // seq_size
    hidden = gate_weight.shape[1] // far
    tok_group = far * tok

    def far_swap(value, step):
        return lax.ppermute(
            value,
            "seq",
            [(i * groups + g, (i ^ step) * groups + g) for i in range(far) for g in range(groups)],
        )

    def gather_far(piece):
        return [piece] + [far_swap(piece, k) for k in range(1, far)]

    def scatter_far(parts):
        total = parts[0].astype(F32)
        for k in reversed(range(1, far)):
            total = total + far_swap(parts[k].astype(LOW), k).astype(F32)
        return total

    def far_exchange(blocks):
        return lax.all_to_all(
            blocks,
            "seq",
            0,
            0,
            axis_index_groups=[[i * groups + g for i in range(far)] for g in range(groups)],
            tiled=True,
        )

    def group_shift(value, step):
        return lax.ppermute(
            value,
            "seq",
            [
                (i * groups + g, i * groups + (g + step) % groups)
                for i in range(far)
                for g in range(groups)
            ],
        )

    def head_swap(value, step):
        return lax.ppermute(value, "head", [(i, i ^ step) for i in range(head_size)])

    flow = Flow()
    gate, plan, got = flow.gate, flow.plan, flow.got

    def keep(name, value, label):
        got[name] = value
        flow.due.setdefault(label, []).append(name)
    half_far = far // 2
    many_rows = half_far * own

    def core_swap(value):
        parts = [value[i : i + own] for i in range(0, value.shape[0], own)]
        return jnp.concatenate([head_swap(part, 1) for part in parts])

    def gather_rows(labels, piece):
        (piece,) = gate(labels[0], [piece])
        parts = gather_far(piece)
        near = jnp.concatenate(
            parts[:half_far] + [head_swap(part, 2) for part in parts[:half_far]]
        )
        (near,) = gate(labels[0] + "n", [near])
        rest = jnp.concatenate(parts[half_far:])
        near, rest = gate(labels[1], [near, rest])
        rest = jnp.concatenate([rest, head_swap(rest, 2)])
        near_got = core_swap(near)
        near, rest, near_got = gate(labels[2], [near, rest, near_got])
        return [
            jnp.concatenate([near, rest]),
            jnp.concatenate([near_got, core_swap(rest)]),
        ]

    def split_rows(chunks):
        return [[c[: 2 * many_rows], c[2 * many_rows :]] for c in chunks]

    def scatter_rows(labels, chunks):
        mine, other = split_rows(chunks)
        *mine, other[0], other[1] = gate(labels[0], mine + other)
        half = mine[1].astype(F32) + core_swap(other[1]).astype(F32)
        kept, sent, *left = gate(
            labels[1], [half[:many_rows], half[many_rows:].astype(LOW), mine[0], other[0]]
        )
        near = left[0].astype(F32) + core_swap(left[1]).astype(F32)
        (near,) = gate(labels[1] + "n", [near])
        rest = kept + head_swap(sent, 2).astype(F32)
        near, near_sent, rest = gate(
            labels[2], [near[:many_rows], near[many_rows:].astype(LOW), rest]
        )
        near = near + head_swap(near_sent, 2).astype(F32)
        (near,) = gate(labels[2] + "n", [near])
        return scatter_far(
            [part[k * own : (k + 1) * own] for part in (near, rest) for k in range(half_far)]
        )

    def plan_gather(tag, piece, far_gates, near_gates, rest_gates):
        plan((tag, "far"), *far_gates, lambda: piece, gather_far)
        halves = (("near", range(half_far), near_gates), ("rest", range(half_far, far), rest_gates))
        for name, ks, gates in halves:
            plan(
                (tag, name),
                *gates,
                lambda ks=ks: jnp.concatenate([got[tag, "far"][k] for k in ks]),
                lambda v: head_swap(v, 2),
            )

        def finish():
            parts = got[tag, "far"]
            mine = parts[:half_far] + [got[tag, "near"]] + parts[half_far:] + [got[tag, "rest"]]
            mine = jnp.concatenate(mine)
            return [mine, core_swap(mine)]

        return finish

    def plan_scatter(tag, chunks, core_gates, rest_gates, near_gates, far_gates):
        made = []

        def halves():
            if not made:
                made.extend(split_rows(chunks()))
            return made

        def half(n):
            mine = halves()[0]
            return mine[n].astype(F32) + got[tag, "core", n].astype(F32)

        def part(k):
            n, at = k // half_far, k % half_far * own
            value = half(n)[:many_rows] + got[tag, "head", n].astype(F32)
            return value[at : at + own].astype(LOW)

        for n, gates in ((1, rest_gates), (0, near_gates)):
            plan((tag, "core", n), *core_gates, lambda n=n: halves()[1][n], core_swap)
            plan(
                (tag, "head", n),
                *gates,
                lambda n=n: half(n)[many_rows:].astype(LOW),
                lambda v: head_swap(v, 2),
            )
        plan(
            (tag, "far"),
            *far_gates,
            lambda: jnp.stack([part(k) for k in range(far)]),
            lambda v: scatter_far([v[k] for k in range(far)]),
        )

    def column_blocks(weight, gain=None):
        breadth = weight.shape[1] // far
        blocks = [weight[:, i * breadth : (i + 1) * breadth] for i in range(far)]
        if gain is not None:
            blocks = [(block.astype(F32) * gain).astype(LOW) for block in blocks]
        return jnp.stack(blocks)

    def row_blocks(weight):
        return weight.reshape(far, weight.shape[0] // far, weight.shape[1]).transpose(0, 2, 1)

    def plan_weight(name, make, breadth, far_gates, group_gates):
        plan(name, *far_gates, make, far_exchange)
        step = breadth // len(group_gates)
        for n, gates in enumerate(group_gates):
            for g in range(1, groups):
                plan(
                    (name, n, g),
                    *gates,
                    lambda n=n: got[name][:, :, n * step : (n + 1) * step],
                    lambda v, g=g: group_shift(v, g),
                )

    def place_weight(name, first, breadth):
        def flat(value):
            return value.reshape(-1, value.shape[2])

        def spot(g):
            return lambda at, i: i * groups + lax.rem(at[2] + groups - g, groups)

        entries = [(flat(got[name]), first, 0, breadth, spot(0))]
        for g in range(1, groups):
            n, start = 0, 0
            while (name, n, g) in got:
                piece = flat(got[name, n, g])
                stop = start + piece.shape[1]
                begin, end = max(first, start), min(first + breadth, stop)
                if begin < end:
                    entries.append((piece, begin - start, begin - first, end - begin, spot(g)))
                n, start = n + 1, stop
        return place(scalars, entries, width, rows_s, breadth)

    def plan_grad(name, make, group_gates, far_gates):
        made = []

        def part(at):
            if not made:
                made.extend(v.reshape(far, groups, rows_s, -1) for v in make())
            return jnp.concatenate(
                [lax.dynamic_index_in_dim(v, at, 1, keepdims=False) for v in made], axis=2
            )

        def total():
            value = part(group_at)
            for g in range(1, groups):
                value = value + got[name, "group", g].astype(F32)
            return value.astype(LOW)

        for g in range(1, groups):
            plan(
                (name, "group", g),
                *group_gates,
                lambda g=g: part((group_at + g) % groups).astype(LOW),
                lambda v, g=g: group_shift(v, g),
            )
        plan(name, *far_gates, total, far_exchange)

    head_spots = [(lambda at, m=m: at[1] ^ m) for m in (0, 2, 1, 3)]

    def every_row(piece):
        half = [piece, head_swap(piece, 2)]
        return half + [head_swap(part, 1) for part in half]

    def head_sum(value):
        value = value + head_swap(value, 1)
        return value + head_swap(value, 2)

    gain_a = attn_gain.astype(F32)[:, None]
    gain_b = mlp_gain.astype(F32)[:, None]

    own_in = lax.dynamic_slice_in_dim(layer_in, head_at * own, own, 0).astype(F32)
    own_grad = lax.dynamic_slice_in_dim(out_grad, head_at * own, own, 0)
    inv_a = inv_rms(own_in)
    normed_a = own_in * inv_a
    plan_weight(
        "attn",
        lambda: jnp.concatenate(
            [column_blocks(w, gain_a) for w in (query_weight, key_weight, value_weight)]
            + [row_blocks(proj_weight)],
            axis=2,
        ),
        4 * HD,
        *G_ATTN,
    )
    plan_weight(
        "mlp",
        lambda: jnp.concatenate(
            [column_blocks(w, gain_b) for w in (gate_weight, up_weight)] + [row_blocks(down_weight)],
            axis=2,
        ),
        3 * hidden,
        *G_MLP,
    )
    finish_top = plan_gather("top", own_grad, *G_TOP)
    gate("start", [])
    far_ids = jnp.arange(far, dtype=jnp.int32)
    positions = (far_ids * groups + group_at)[:, None] * tok + jnp.arange(tok, dtype=jnp.int32)
    frequency = ROPE_BASE ** (-jnp.arange(HD // 2, dtype=F32) * 2.0 / HD)
    angles = positions.reshape(tok_group).astype(F32)[:, None] * frequency[None, :]
    cosine, sine_tab = jnp.cos(angles), jnp.sin(angles)
    cosine = jnp.concatenate([cosine, cosine], axis=1)
    signed = jnp.concatenate([-sine_tab, sine_tab], axis=1)
    docs = doc_ids.reshape(far, groups, tok)
    query_doc = lax.dynamic_index_in_dim(docs, group_at, 1, keepdims=False).reshape(tok_group, 1)
    key_doc = jnp.stack(
        [
            lax.dynamic_index_in_dim(docs, (group_at - g) % groups, 1, keepdims=False).reshape(
                tok_group
            )
            for g in range(groups)
        ]
    )
    keep("tables", (cosine, signed, query_doc, key_doc), "x0n")
    hidden_a = gather_rows(("x0", "x1", "x2"), normed_a.astype(LOW))
    qkv_full, proj_turned = place_weight("attn", 0, 3 * HD), place_weight("attn", 3 * HD, HD)

    cosine, signed, query_doc, key_doc = got["tables"]
    hidden_a = gate("qkv", hidden_a)
    query_rot, key_own = rotate_all(
        scalars, [dot(h, qkv_full) for h in hidden_a], cosine, signed, far, head_size, own
    )
    key_own, query_rot = gate("kv", [key_own, query_rot])
    keys = [key_own] + [group_shift(key_own, g) for g in range(1, groups)]

    query_rot, *keys = gate("attend", [query_rot] + keys)
    attn_low = attend(scalars, query_rot, keys, query_doc, key_doc, far, head_size, own)
    middle = own_in + scatter_rows(("z0", "z1", "z2"), [dot_last(a, proj_turned).astype(LOW) for a in attn_low])

    inv_b = inv_rms(middle)
    normed_b = middle * inv_b
    hidden_b = gather_rows(("h0", "h1", "h2"), normed_b.astype(LOW))
    hidden_b = gate("mlp", hidden_b)
    gate_up = place_weight("mlp", 0, 2 * hidden)
    down_turned = place_weight("mlp", 2 * hidden, hidden)
    parts, active = [], []
    for h in hidden_b:
        gate_up_val = dot(h, gate_up)
        gate_val, up_val = gate_up_val[:, :hidden], gate_up_val[:, hidden:]
        gate_sig = jax.nn.sigmoid(gate_val)
        silu_val = gate_val * gate_sig
        active.append((silu_val * up_val).astype(LOW))
        parts.append(
            (silu_val, up_val * gate_sig * (1.0 + gate_val * (1.0 - gate_sig)))
        )
    plan_scatter(
        "out", lambda: [dot_last(a, down_turned).astype(LOW) for a in active], *G_OUT
    )
    grad_top = finish_top()
    grad_gu = []
    for top, (silu_val, gate_slope) in zip(grad_top, parts):
        grad_active = dot(top, down_turned)
        grad_gu.append(
            jnp.concatenate(
                [(grad_active * gate_slope).astype(LOW), (grad_active * silu_val).astype(LOW)],
                axis=1,
            )
        )

    def over_tokens(left_mats, right_mats):
        return sum(dot_first(a, b) for a, b in zip(left_mats, right_mats))

    keep("mlp kept", (hidden_b, grad_gu, grad_top, active), "g1n")

    def mlp_grads():
        hidden_b, grad_gu, grad_top, active = got["mlp kept"]
        return [over_tokens(hidden_b, grad_gu), over_tokens(grad_top, active)]

    plan_grad("mlp grads", mlp_grads, *G_GRAD_MLP)
    grad_normed_b = scatter_rows(
        ("g0", "g1", "g2"),
        [
            dot_last(g, gate_up).astype(LOW) for g in grad_gu
        ],
    )
    grad_middle = own_grad.astype(F32) + norm_back(grad_normed_b, normed_b, inv_b)
    grad_mix = gather_rows(("m0", "m1", "m2"), grad_middle.astype(LOW))

    grad_mix = gate("back", grad_mix)
    grad_attn = [dot(g, proj_turned).astype(LOW) for g in grad_mix]
    grad_query, *grad_keys = attend_back(
        scalars, query_rot, keys, query_doc, key_doc, grad_attn, far, head_size, own
    )
    grad_query, *grad_keys = gate("kvb", [grad_query] + grad_keys)
    grad_keys = [grad_keys[0]] + [
        group_shift(grad_keys[g], groups - g) for g in range(1, groups)
    ]
    grad_query, *grad_keys = gate("turn", [grad_query] + grad_keys)
    grad_qkv = rotate_back(
        scalars, grad_query, grad_keys, cosine, signed, far, head_size, own
    )
    keep("attn kept", (hidden_a, grad_qkv, grad_mix, attn_low), "r1")

    def attn_grads():
        hidden_a, grad_qkv, grad_mix, attn_low = got["attn kept"]
        return [over_tokens(hidden_a, grad_qkv), over_tokens(grad_mix, attn_low)]

    plan_grad("attn grads", attn_grads, *G_GRAD_ATTN)
    grad_normed_a = scatter_rows(
        ("r0", "r1", "r2"), [dot_last(g, qkv_full).astype(LOW) for g in grad_qkv]
    )
    grad_in = (grad_middle + norm_back(grad_normed_a, normed_a, inv_a)).astype(LOW)

    (grad_in,) = gate("in", [grad_in])
    in_rows = every_row(grad_in)
    in_rows = gate("end", in_rows)
    out_rows = every_row((middle + got["out", "far"]).astype(LOW))
    grad_gate, grad_up, grad_down, mlp_terms = finish_weights(
        scalars, got["mlp grads"], [gate_weight, up_weight], gain_b
    )
    grad_query_w, grad_key_w, grad_value_w, grad_proj, attn_terms = finish_weights(
        scalars, got["attn grads"], [query_weight, key_weight, value_weight], gain_a
    )
    layer_out = place_wide(scalars, out_rows, head_spots, tok, width, LOW)
    input_grad = place_wide(scalars, in_rows, head_spots, tok, width)
    terms = head_sum(jnp.concatenate([attn_terms, mlp_terms], axis=1).T)
    return (
        layer_out,
        input_grad,
        grad_query_w,
        grad_key_w,
        grad_value_w,
        grad_proj,
        grad_gate,
        grad_up,
        grad_down,
        terms[0],
        terms[1],
    )


def solution(mesh):
    return jax.shard_map(
        local,
        mesh=mesh,
        in_specs=(
            P("seq", None),
            P("seq", None),
            P(),
            P("seq"),
            P("seq", "head"),
            P("seq", "head"),
            P("seq", "head"),
            P("head", "seq"),
            P("seq"),
            P("seq", "head"),
            P("seq", "head"),
            P("head", "seq"),
        ),
        out_specs=(
            P("seq", None),
            P("seq", None),
            P("seq", "head"),
            P("seq", "head"),
            P("seq", "head"),
            P("head", "seq"),
            P("seq", "head"),
            P("seq", "head"),
            P("head", "seq"),
            P("seq"),
            P("seq"),
        ),
        check_vma=False,
    )
```

```python
import functools
import math

import jax
import jax.numpy as jnp
from jax import lax
from jax.experimental import pallas as pl
from jax.experimental.pallas import tpu as pltpu
from jax.sharding import PartitionSpec as P

HD = 128
EPSILON = 1e-05
ROPE_BASE = 10000.0
LOG_BIAS = math.log(4096.0)
LOW = jnp.bfloat16
F32 = jnp.float32
G_ATTN = (("start", "x1"), [("x1", "x2")])
G_TOP = (("z1n", "z2n"), ("z2n", "h0"), ("z2n", "h1"))
G_MLP = (("x1", "z1"), [("z1", "z2n"), ("z2n", "h1")])
G_GRAD_MLP = (("g2", "m2"), ("back", "r2n"))
G_OUT = (("m0", "m1"), ("m1", "kvb"), ("m2", "kvb"), ("r2n", "end"))
G_GRAD_ATTN = (("r1n", "r2n"), ("r2n", "end"))
VMEM_ASK = 40 * 1024 * 1024


def dot(left_mat, right_mat):
    return lax.dot_general(
        left_mat, right_mat, (((1,), (0,)), ((), ())), preferred_element_type=F32
    )


def dot_last(left_mat, right_mat):
    return lax.dot_general(
        left_mat, right_mat, (((1,), (1,)), ((), ())), preferred_element_type=F32
    )


def dot_first(left_mat, right_mat):
    return lax.dot_general(
        left_mat, right_mat, (((0,), (0,)), ((), ())), preferred_element_type=F32
    )


def inv_rms(values):
    return lax.rsqrt(jnp.mean(values * values, axis=-1, keepdims=True) + EPSILON)


def norm_back(grad_normed, normed, inv_root):
    return inv_root * (
        grad_normed - normed * jnp.mean(grad_normed * normed, axis=-1, keepdims=True)
    )


def pick(stacked, index):
    return lax.dynamic_index_in_dim(stacked, index, 0, keepdims=False)


class Flow:
    def __init__(self):
        self.plans, self.got, self.due = {}, {}, {}

    def plan(self, name, start, end, make, send):
        self.plans.setdefault(start, []).append((name, end, make, send))

    def gate(self, label, values):
        planned = self.plans.pop(label, [])
        names = self.due.pop(label, [])
        ended = [self.got[name] for name in names]
        values, ended, operands = lax.optimization_barrier(
            (list(values), ended, [make() for _, _, make, _ in planned])
        )
        self.got.update(zip(names, ended))
        for (name, end, _, send), operand in zip(planned, operands):
            self.got[name] = send(operand)
            self.due.setdefault(end, []).append(name)
        return values


def shape_of(rows, cols, kind):
    return jax.ShapeDtypeStruct((rows, cols), kind)


def at_rows(index, count):
    return pl.ds(pl.multiple_of(index * count, count), count)


SMEM_SPEC = pl.BlockSpec(memory_space=pltpu.SMEM)
ANY_SPEC = pl.BlockSpec(memory_space=pl.ANY)
VMEM_SPEC = pl.BlockSpec(memory_space=pltpu.VMEM)


def call(body, outs, scalars, arrays, scratch=(), space=VMEM_SPEC, flops=0):
    outs = tuple(outs)
    moved = sum(math.prod(a.shape) * a.dtype.itemsize for a in tuple(arrays) + outs)
    return pl.pallas_call(
        body,
        out_shape=outs,
        in_specs=[SMEM_SPEC] + [space] * len(arrays),
        out_specs=tuple([space] * len(outs)),
        scratch_shapes=list(scratch),
        compiler_params=pltpu.CompilerParams(vmem_limit_bytes=VMEM_ASK),
        cost_estimate=pl.CostEstimate(flops=flops, bytes_accessed=moved, transcendentals=0),
    )(scalars, *arrays)


def place(scalars, entries, rows, height, breadth):
    number = len(entries)
    blocks = entries[0][0].shape[0] // height

    def body(at, *refs):
        ins, out, sems = refs[:number], refs[number], refs[number + 1]
        copies = []
        for n, (_, first, target, count, spot) in enumerate(entries):
            for i in range(blocks):
                copies.append(
                    pltpu.make_async_copy(
                        ins[n].at[i * height : (i + 1) * height, first : first + count],
                        out.at[at_rows(spot(at, i), height), target : target + count],
                        sems.at[n * blocks + i],
                    )
                )
        for copy in copies:
            copy.start()
        for copy in copies:
            copy.wait()

    return call(
        body,
        [shape_of(rows, breadth, LOW)],
        scalars,
        [entry[0] for entry in entries],
        [pltpu.SemaphoreType.DMA((number * blocks,))],
        ANY_SPEC,
    )[0]


def place_wide(scalars, pieces, spots, rows, cols, kind=F32):
    count = len(pieces)

    def body(at, *refs):
        out = refs[count]
        for n in range(count):
            out[at_rows(spots[n](at), pieces[n].shape[0]), :] = refs[n][...].astype(kind)

    return call(body, [shape_of(rows, cols, kind)], scalars, pieces)[0]


def finish_weights(scalars, pieces, weights, gain):
    many = len(weights)
    height, breadth = weights[0].shape
    count, block = pieces.shape[0], pieces.shape[2] // (many + 1)

    def body(at, piece_ref, *refs):
        held, gains = refs[:many], refs[many]
        outs, turned, terms = refs[many + 1 : -2], refs[-2], refs[-1]
        total = jnp.zeros((height, 1), F32)
        scale = gains[...]
        for i in range(count):
            where = slice(i * block, (i + 1) * block)
            for m in range(many):
                grad = piece_ref[i, :, m * block : (m + 1) * block].astype(F32)
                outs[m][:, where] = grad * scale
                total += jnp.sum(grad * held[m][:, where].astype(F32), axis=1, keepdims=True)
            turned[where, :] = piece_ref[i, :, many * block :].astype(F32).T
        terms[...] = total

    outs = [shape_of(height, breadth, F32) for _ in weights]
    outs += [shape_of(breadth, height, F32), shape_of(height, 1, F32)]
    return call(body, outs, scalars, [pieces] + list(weights) + [gain])


def turn(values, cosine, signed):
    return values * cosine + pltpu.roll(values, HD // 2, 1) * signed


def piece_spots(far, head_size, own):
    for c in range(2):
        row = 0
        for first in (0, far // 2):
            for y in range(head_size // 2):
                for k in range(first, first + far // 2):
                    yield c, row, k, 2 * y + c
                    row += own


def rotate_all(scalars, chunks, cosine, signed, far, head_size, own):
    tok = own * head_size

    def body(at, low_ref, high_ref, cos_ref, sin_ref, query_ref, kv_ref):
        ins = (low_ref, high_ref)
        for c, row, k, m in piece_spots(far, head_size, own):
            spot = pl.ds(
                pl.multiple_of((at[0] ^ k) * tok + (at[1] ^ m) * own, own), own
            )
            cos_rows, sin_rows = cos_ref[spot, :], sin_ref[spot, :]
            value = ins[c][row : row + own, :]
            query_ref[spot, :] = turn(value[:, :HD], cos_rows, sin_rows).astype(LOW)
            kv_ref[spot, :HD] = turn(value[:, HD : 2 * HD], cos_rows, sin_rows).astype(LOW)
            kv_ref[spot, HD:] = value[:, 2 * HD :].astype(LOW)

    rows = far * tok
    return call(
        body,
        [shape_of(rows, HD, LOW), shape_of(rows, 2 * HD, LOW)],
        scalars,
        list(chunks) + [cosine, signed],
    )


def live_pairs(at, groups, far, tok):
    for i in range(far):
        for g in range(groups):
            for j in range(i + 1):
                yield i, g, j


def probabilities(at, query, key, query_doc, key_doc, i, g, j, groups):
    scores = lax.dot_general(query, key, (((1,), (1,)), ((), ())), preferred_element_type=F32)
    live = query_doc == key_doc
    if i == j:
        if g == 0:
            rows = lax.broadcasted_iota(jnp.int32, scores.shape, 0)
            cols = lax.broadcasted_iota(jnp.int32, scores.shape, 1)
            live = live & (rows >= cols)
        else:
            source = lax.rem(at[2] - g + groups, groups)
            live = live & (query_doc >= jnp.where(source < at[2], 0, 1 << 30))
    return jnp.where(live, jax.nn.sigmoid(scores * HD**-0.5 - LOG_BIAS), 0.0)


def attend(scalars, query, keys, query_doc, key_doc, far, head_size, own):
    tok, groups = own * head_size, len(keys)

    def body(at, query_ref, doc_ref, key_doc_ref, *refs):
        key_refs, (low_ref, high_ref, held) = refs[:groups], refs[groups:]
        for i in range(far):
            block = query_ref[i * tok : (i + 1) * tok, :]
            docs = doc_ref[i * tok : (i + 1) * tok, :]
            total = jnp.zeros((tok, HD), F32)
            for j in range(i + 1):
                for g in range(groups):
                    span = slice(j * tok, (j + 1) * tok)
                    probs = probabilities(
                        at, block, key_refs[g][span, :HD], docs, key_doc_ref[g : g + 1, span], i, g, j, groups
                    )
                    total += dot(probs.astype(LOW), key_refs[g][span, HD:])
            held[i * tok : (i + 1) * tok, :] = total.astype(LOW)
        outs = (low_ref, high_ref)
        for c, row, k, m in piece_spots(far, head_size, own):
            spot = pl.ds(
                pl.multiple_of((at[0] ^ k) * tok + (at[1] ^ m) * own, own), own
            )
            outs[c][row : row + own, :] = held[spot, :]

    rows = far * tok
    return call(
        body,
        [shape_of(rows // 2, HD, LOW)] * 2,
        scalars,
        [query, query_doc, key_doc] + list(keys),
        [pltpu.VMEM((rows, HD), LOW)],
        flops=4 * rows * rows * groups * HD // 2,
    )


def attend_back(scalars, query, keys, query_doc, key_doc, grads, far, head_size, own):
    tok, groups = own * head_size, len(keys)

    def body(at, query_ref, doc_ref, key_doc_ref, low_ref, high_ref, *refs):
        key_refs, outs, held = refs[:groups], refs[groups:-1], refs[-1]
        query_out, key_outs = outs[0], outs[1:]
        ins = (low_ref, high_ref)
        for c, row, k, m in piece_spots(far, head_size, own):
            spot = pl.ds(
                pl.multiple_of((at[0] ^ k) * tok + (at[1] ^ m) * own, own), own
            )
            held[spot, :] = ins[c][row : row + own, :]
        for j in range(far):
            for g in range(groups):
                span = slice(j * tok, (j + 1) * tok)
                key, value = key_refs[g][span, :HD], key_refs[g][span, HD:]
                key_total = jnp.zeros((tok, HD), F32)
                value_total = jnp.zeros((tok, HD), F32)
                for i in range(j, far):
                    rows = slice(i * tok, (i + 1) * tok)
                    block, grad = query_ref[rows, :], held[rows, :]
                    probs = probabilities(
                        at, block, key, doc_ref[rows, :], key_doc_ref[g : g + 1, span], i, g, j, groups
                    )
                    value_total += dot_first(probs.astype(LOW), grad)
                    terms = (dot_last(grad, value) * probs * (1.0 - probs)).astype(LOW)
                    key_total += dot_first(terms, block)
                    part = dot(terms, key) * HD**-0.5
                    if j == 0 and g == 0:
                        query_out[rows, :] = part
                    else:
                        query_out[rows, :] += part
                kind = key_outs[g].dtype
                key_outs[g][span, :HD] = (key_total * HD**-0.5).astype(kind)
                key_outs[g][span, HD:] = value_total.astype(kind)

    rows = far * tok
    return call(
        body,
        [shape_of(rows, HD, F32), shape_of(rows, 2 * HD, F32)]
        + [shape_of(rows, 2 * HD, LOW)] * (groups - 1),
        scalars,
        [query, query_doc, key_doc] + list(grads) + list(keys),
        [pltpu.VMEM((rows, HD), LOW)],
        flops=10 * rows * rows * groups * HD // 2,
    )


def rotate_back(scalars, query, keys, cosine, signed, far, head_size, own):
    tok, count = own * head_size, len(keys)

    def body(at, query_ref, cos_ref, sin_ref, *refs):
        key_refs, outs = refs[:count], refs[count:]
        for c, row, k, m in piece_spots(far, head_size, own):
            spot = pl.ds(
                pl.multiple_of((at[0] ^ k) * tok + (at[1] ^ m) * own, own), own
            )
            cos_rows, sin_rows = cos_ref[spot, :], -sin_ref[spot, :]
            total = key_refs[0][spot, :]
            for ref in key_refs[1:]:
                total += ref[spot, :].astype(F32)
            rows = slice(row, row + own)
            outs[c][rows, :HD] = turn(query_ref[spot, :], cos_rows, sin_rows).astype(LOW)
            outs[c][rows, HD : 2 * HD] = turn(total[:, :HD], cos_rows, sin_rows).astype(LOW)
            outs[c][rows, 2 * HD :] = total[:, HD:].astype(LOW)

    rows = far * tok
    return call(
        body,
        [shape_of(rows // 2, 3 * HD, LOW)] * 2,
        scalars,
        [query, cosine, signed] + list(keys),
    )


def local(
    layer_in,
    out_grad,
    doc_ids,
    attn_gain,
    query_weight,
    key_weight,
    value_weight,
    proj_weight,
    mlp_gain,
    gate_weight,
    up_weight,
    down_weight,
):
    tok, width = layer_in.shape
    seq_size, head_size = lax.axis_size("seq"), lax.axis_size("head")
    far = query_weight.shape[1] // HD
    groups = seq_size // far
    own = tok // head_size
    seq_at, head_at = lax.axis_index("seq"), lax.axis_index("head")
    far_at, group_at = seq_at // groups, seq_at % groups
    scalars = jnp.stack([far_at, head_at, group_at]).astype(jnp.int32)
    rows_s = width // seq_size
    hidden = gate_weight.shape[1] // far
    tok_group = far * tok

    def far_swap(value, step):
        return lax.ppermute(
            value,
            "seq",
            [(i * groups + g, (i ^ step) * groups + g) for i in range(far) for g in range(groups)],
        )

    def gather_far(piece):
        return [piece] + [far_swap(piece, k) for k in range(1, far)]

    def scatter_far(parts):
        total = parts[0].astype(F32)
        for k in reversed(range(1, far)):
            total = total + far_swap(parts[k].astype(LOW), k).astype(F32)
        return total

    def far_exchange(blocks):
        return lax.all_to_all(
            blocks,
            "seq",
            0,
            0,
            axis_index_groups=[[i * groups + g for i in range(far)] for g in range(groups)],
            tiled=True,
        )

    def group_shift(value, step):
        return lax.ppermute(
            value,
            "seq",
            [
                (i * groups + g, i * groups + (g + step) % groups)
                for i in range(far)
                for g in range(groups)
            ],
        )

    def head_swap(value, step):
        return lax.ppermute(value, "head", [(i, i ^ step) for i in range(head_size)])

    flow = Flow()
    gate, plan, got = flow.gate, flow.plan, flow.got

    def keep(name, value, label):
        got[name] = value
        flow.due.setdefault(label, []).append(name)
    half_far = far // 2
    many_rows = half_far * own

    def core_swap(value):
        parts = [value[i : i + own] for i in range(0, value.shape[0], own)]
        return jnp.concatenate([head_swap(part, 1) for part in parts])

    def gather_rows(labels, piece, split=True):
        (piece,) = gate(labels[0], [piece])
        parts = gather_far(piece)
        if not split:
            (mine,) = gate(labels[1], [jnp.concatenate(parts)])
            other = head_swap(mine, 2)
            near, rest = slice(0, many_rows), slice(many_rows, None)
            mine, other = gate(labels[2], [mine, other])
            half = [jnp.concatenate([mine[rows], other[rows]]) for rows in (near, rest)]
            return [jnp.concatenate(half), jnp.concatenate([core_swap(part) for part in half])]
        near = jnp.concatenate(
            parts[:half_far] + [head_swap(part, 2) for part in parts[:half_far]]
        )
        (near,) = gate(labels[0] + "n", [near])
        rest = jnp.concatenate(parts[half_far:])
        near, rest = gate(labels[1], [near, rest])
        rest = jnp.concatenate([rest, head_swap(rest, 2)])
        near_got = core_swap(near)
        near, rest, near_got = gate(labels[2], [near, rest, near_got])
        return [
            jnp.concatenate([near, rest]),
            jnp.concatenate([near_got, core_swap(rest)]),
        ]

    def split_rows(chunks):
        return [[c[: 2 * many_rows], c[2 * many_rows :]] for c in chunks]

    def scatter_rows(labels, chunks):
        mine, other = split_rows(chunks)
        *mine, other[0], other[1] = gate(labels[0], mine + other)
        half = mine[1].astype(F32) + core_swap(other[1]).astype(F32)
        kept, sent, *left = gate(
            labels[1], [half[:many_rows], half[many_rows:].astype(LOW), mine[0], other[0]]
        )
        near = left[0].astype(F32) + core_swap(left[1]).astype(F32)
        (near,) = gate(labels[1] + "n", [near])
        rest = kept + head_swap(sent, 2).astype(F32)
        near, near_sent, rest = gate(
            labels[2], [near[:many_rows], near[many_rows:].astype(LOW), rest]
        )
        near = near + head_swap(near_sent, 2).astype(F32)
        (near,) = gate(labels[2] + "n", [near])
        return scatter_far(
            [part[k * own : (k + 1) * own] for part in (near, rest) for k in range(half_far)]
        )

    def plan_gather(tag, piece, far_gates, near_gates, rest_gates):
        plan((tag, "far"), *far_gates, lambda: piece, gather_far)
        halves = (("near", range(half_far), near_gates), ("rest", range(half_far, far), rest_gates))
        for name, ks, gates in halves:
            plan(
                (tag, name),
                *gates,
                lambda ks=ks: jnp.concatenate([got[tag, "far"][k] for k in ks]),
                lambda v: head_swap(v, 2),
            )

        def finish():
            parts = got[tag, "far"]
            mine = parts[:half_far] + [got[tag, "near"]] + parts[half_far:] + [got[tag, "rest"]]
            mine = jnp.concatenate(mine)
            return [mine, core_swap(mine)]

        return finish

    def plan_scatter(tag, chunks, core_gates, rest_gates, near_gates, far_gates):
        made = []

        def halves():
            if not made:
                made.extend(split_rows(chunks()))
            return made

        def half(n):
            mine = halves()[0]
            return mine[n].astype(F32) + got[tag, "core", n].astype(F32)

        def part(k):
            n, at = k // half_far, k % half_far * own
            value = half(n)[:many_rows] + got[tag, "head", n].astype(F32)
            return value[at : at + own].astype(LOW)

        for n, gates in ((1, rest_gates), (0, near_gates)):
            plan((tag, "core", n), *core_gates, lambda n=n: halves()[1][n], core_swap)
            plan(
                (tag, "head", n),
                *gates,
                lambda n=n: half(n)[many_rows:].astype(LOW),
                lambda v: head_swap(v, 2),
            )
        plan(
            (tag, "far"),
            *far_gates,
            lambda: jnp.stack([part(k) for k in range(far)]),
            lambda v: scatter_far([v[k] for k in range(far)]),
        )

    def column_blocks(weight, gain=None):
        breadth = weight.shape[1] // far
        blocks = [weight[:, i * breadth : (i + 1) * breadth] for i in range(far)]
        if gain is not None:
            blocks = [(block.astype(F32) * gain).astype(LOW) for block in blocks]
        return jnp.stack(blocks)

    def row_blocks(weight):
        return weight.reshape(far, weight.shape[0] // far, weight.shape[1]).transpose(0, 2, 1)

    def plan_weight(name, make, breadth, far_gates, group_gates):
        plan(name, *far_gates, make, far_exchange)
        step = breadth // len(group_gates)
        for n, gates in enumerate(group_gates):
            for g in range(1, groups):
                plan(
                    (name, n, g),
                    *gates,
                    lambda n=n: got[name][:, :, n * step : (n + 1) * step],
                    lambda v, g=g: group_shift(v, g),
                )

    def place_weight(name, first, breadth):
        def flat(value):
            return value.reshape(-1, value.shape[2])

        def spot(g):
            return lambda at, i: i * groups + lax.rem(at[2] + groups - g, groups)

        entries = [(flat(got[name]), first, 0, breadth, spot(0))]
        for g in range(1, groups):
            n, start = 0, 0
            while (name, n, g) in got:
                piece = flat(got[name, n, g])
                stop = start + piece.shape[1]
                begin, end = max(first, start), min(first + breadth, stop)
                if begin < end:
                    entries.append((piece, begin - start, begin - first, end - begin, spot(g)))
                n, start = n + 1, stop
        return place(scalars, entries, width, rows_s, breadth)

    def plan_grad(name, make, group_gates, far_gates):
        made = []

        def part(at):
            if not made:
                made.extend(v.reshape(far, groups, rows_s, -1) for v in make())
            return jnp.concatenate(
                [lax.dynamic_index_in_dim(v, at, 1, keepdims=False) for v in made], axis=2
            )

        def total():
            value = part(group_at)
            for g in range(1, groups):
                value = value + got[name, "group", g].astype(F32)
            return value.astype(LOW)

        for g in range(1, groups):
            plan(
                (name, "group", g),
                *group_gates,
                lambda g=g: part((group_at + g) % groups).astype(LOW),
                lambda v, g=g: group_shift(v, g),
            )
        plan(name, *far_gates, total, far_exchange)

    head_spots = [(lambda at, m=m: at[1] ^ m) for m in (0, 2, 1, 3)]

    def every_row(piece):
        half = [piece, head_swap(piece, 2)]
        return half + [head_swap(part, 1) for part in half]

    def head_sum(value):
        value = value + head_swap(value, 1)
        return value + head_swap(value, 2)

    gain_a = attn_gain.astype(F32)[:, None]
    gain_b = mlp_gain.astype(F32)[:, None]

    own_in = lax.dynamic_slice_in_dim(layer_in, head_at * own, own, 0).astype(F32)
    own_grad = lax.dynamic_slice_in_dim(out_grad, head_at * own, own, 0)
    inv_a = inv_rms(own_in)
    normed_a = own_in * inv_a
    plan_weight(
        "attn",
        lambda: jnp.concatenate(
            [column_blocks(w, gain_a) for w in (query_weight, key_weight, value_weight)]
            + [row_blocks(proj_weight)],
            axis=2,
        ),
        4 * HD,
        *G_ATTN,
    )
    plan_weight(
        "mlp",
        lambda: jnp.concatenate(
            [column_blocks(w, gain_b) for w in (gate_weight, up_weight)] + [row_blocks(down_weight)],
            axis=2,
        ),
        3 * hidden,
        *G_MLP,
    )
    finish_top = plan_gather("top", own_grad, *G_TOP)
    gate("start", [])
    far_ids = jnp.arange(far, dtype=jnp.int32)
    positions = (far_ids * groups + group_at)[:, None] * tok + jnp.arange(tok, dtype=jnp.int32)
    frequency = ROPE_BASE ** (-jnp.arange(HD // 2, dtype=F32) * 2.0 / HD)
    angles = positions.reshape(tok_group).astype(F32)[:, None] * frequency[None, :]
    cosine, sine_tab = jnp.cos(angles), jnp.sin(angles)
    cosine = jnp.concatenate([cosine, cosine], axis=1)
    signed = jnp.concatenate([-sine_tab, sine_tab], axis=1)
    docs = doc_ids.reshape(far, groups, tok)
    query_doc = lax.dynamic_index_in_dim(docs, group_at, 1, keepdims=False).reshape(tok_group, 1)
    key_doc = jnp.stack(
        [
            lax.dynamic_index_in_dim(docs, (group_at - g) % groups, 1, keepdims=False).reshape(
                tok_group
            )
            for g in range(groups)
        ]
    )
    keep("tables", (cosine, signed, query_doc, key_doc), "x0n")
    hidden_a = gather_rows(("x0", "x1", "x2"), normed_a.astype(LOW))
    qkv_full, proj_turned = place_weight("attn", 0, 3 * HD), place_weight("attn", 3 * HD, HD)

    cosine, signed, query_doc, key_doc = got["tables"]
    hidden_a = gate("qkv", hidden_a)
    query_rot, key_own = rotate_all(
        scalars, [dot(h, qkv_full) for h in hidden_a], cosine, signed, far, head_size, own
    )
    key_own, query_rot = gate("kv", [key_own, query_rot])
    keys = [key_own] + [group_shift(key_own, g) for g in range(1, groups)]

    query_rot, *keys = gate("attend", [query_rot] + keys)
    attn_low = attend(scalars, query_rot, keys, query_doc, key_doc, far, head_size, own)
    middle = own_in + scatter_rows(("z0", "z1", "z2"), [dot_last(a, proj_turned).astype(LOW) for a in attn_low])

    inv_b = inv_rms(middle)
    normed_b = middle * inv_b
    hidden_b = gather_rows(("h0", "h1", "h2"), normed_b.astype(LOW))
    hidden_b = gate("mlp", hidden_b)
    gate_up = place_weight("mlp", 0, 2 * hidden)
    down_turned = place_weight("mlp", 2 * hidden, hidden)
    parts, active = [], []
    for h in hidden_b:
        gate_up_val = dot(h, gate_up)
        gate_val, up_val = gate_up_val[:, :hidden], gate_up_val[:, hidden:]
        gate_sig = jax.nn.sigmoid(gate_val)
        silu_val = gate_val * gate_sig
        active.append((silu_val * up_val).astype(LOW))
        parts.append(
            (silu_val, up_val * gate_sig * (1.0 + gate_val * (1.0 - gate_sig)))
        )
    plan_scatter(
        "out", lambda: [dot_last(a, down_turned).astype(LOW) for a in active], *G_OUT
    )
    grad_top = finish_top()
    grad_gu = []
    for top, (silu_val, gate_slope) in zip(grad_top, parts):
        grad_active = dot(top, down_turned)
        grad_gu.append(
            jnp.concatenate(
                [(grad_active * gate_slope).astype(LOW), (grad_active * silu_val).astype(LOW)],
                axis=1,
            )
        )

    def over_tokens(left_mats, right_mats):
        return sum(dot_first(a, b) for a, b in zip(left_mats, right_mats))

    keep("mlp kept", (hidden_b, grad_gu, grad_top, active), "g1n")

    def mlp_grads():
        hidden_b, grad_gu, grad_top, active = got["mlp kept"]
        return [over_tokens(hidden_b, grad_gu), over_tokens(grad_top, active)]

    plan_grad("mlp grads", mlp_grads, *G_GRAD_MLP)
    grad_normed_b = scatter_rows(
        ("g0", "g1", "g2"),
        [
            dot_last(g, gate_up).astype(LOW) for g in grad_gu
        ],
    )
    grad_middle = own_grad.astype(F32) + norm_back(grad_normed_b, normed_b, inv_b)
    grad_mix = gather_rows(("m0", "m1", "m2"), grad_middle.astype(LOW), False)

    grad_mix = gate("back", grad_mix)
    grad_attn = [dot(g, proj_turned).astype(LOW) for g in grad_mix]
    grad_query, *grad_keys = attend_back(
        scalars, query_rot, keys, query_doc, key_doc, grad_attn, far, head_size, own
    )
    grad_query, *grad_keys = gate("kvb", [grad_query] + grad_keys)
    grad_keys = [grad_keys[0]] + [
        group_shift(grad_keys[g], groups - g) for g in range(1, groups)
    ]
    grad_query, *grad_keys = gate("turn", [grad_query] + grad_keys)
    grad_qkv = rotate_back(
        scalars, grad_query, grad_keys, cosine, signed, far, head_size, own
    )
    keep("attn kept", (hidden_a, grad_qkv, grad_mix, attn_low), "r1")

    def attn_grads():
        hidden_a, grad_qkv, grad_mix, attn_low = got["attn kept"]
        return [over_tokens(hidden_a, grad_qkv), over_tokens(grad_mix, attn_low)]

    plan_grad("attn grads", attn_grads, *G_GRAD_ATTN)
    grad_normed_a = scatter_rows(
        ("r0", "r1", "r2"), [dot_last(g, qkv_full).astype(LOW) for g in grad_qkv]
    )
    grad_in = (grad_middle + norm_back(grad_normed_a, normed_a, inv_a)).astype(LOW)

    (grad_in,) = gate("in", [grad_in])
    in_rows = every_row(grad_in)
    in_rows = gate("end", in_rows)
    out_rows = every_row((middle + got["out", "far"]).astype(LOW))
    grad_gate, grad_up, grad_down, mlp_terms = finish_weights(
        scalars, got["mlp grads"], [gate_weight, up_weight], gain_b
    )
    grad_query_w, grad_key_w, grad_value_w, grad_proj, attn_terms = finish_weights(
        scalars, got["attn grads"], [query_weight, key_weight, value_weight], gain_a
    )
    layer_out = place_wide(scalars, out_rows, head_spots, tok, width, LOW)
    input_grad = place_wide(scalars, in_rows, head_spots, tok, width)
    terms = head_sum(jnp.concatenate([attn_terms, mlp_terms], axis=1).T)
    return (
        layer_out,
        input_grad,
        grad_query_w,
        grad_key_w,
        grad_value_w,
        grad_proj,
        grad_gate,
        grad_up,
        grad_down,
        terms[0],
        terms[1],
    )


def solution(mesh):
    return jax.shard_map(
        local,
        mesh=mesh,
        in_specs=(
            P("seq", None),
            P("seq", None),
            P(),
            P("seq"),
            P("seq", "head"),
            P("seq", "head"),
            P("seq", "head"),
            P("head", "seq"),
            P("seq"),
            P("seq", "head"),
            P("seq", "head"),
            P("head", "seq"),
        ),
        out_specs=(
            P("seq", None),
            P("seq", None),
            P("seq", "head"),
            P("seq", "head"),
            P("seq", "head"),
            P("head", "seq"),
            P("seq", "head"),
            P("seq", "head"),
            P("head", "seq"),
            P("seq"),
            P("seq"),
        ),
        check_vma=False,
    )
```
